256 devices in a mesh: gx: 8 (over z), gy: 4 (over y_lo, core), gz: 8 (over x, y_hi).
Axes of the slice: x: 4, y: 4 (y_hi: 2, y_lo: 2; y = y_hi * 2 + y_lo), z: 8, core: 2. Of those that a mesh axis runs over, the one named last changes fastest.
Arguments:
- tokens: bfloat16 [768, 6144], P(('gy', 'gx'), 'gz'), may hold values from -6 to 6
- gain: float32 [6144], P('gz'), may hold values from 0.5 to 1.5
- w_in: bfloat16 [6144, 24576], P('gz', ('gx', 'gy')), may hold values from -0.078125 to 0.078125
- b_in: float32 [24576], P('gx'), may hold values from -4 to 4
- w_out: bfloat16 [24576, 6144], P('gx', ('gz', 'gy')), may hold values from -0.0390625 to 0.0390625
- cotangent: bfloat16 [768, 6144], P(('gy', 'gx'), 'gz'), may hold values from -6 to 6
Outputs:
- y_branch: bfloat16 [768, 6144], P(('gy', 'gx'), 'gz')
- input_grad: bfloat16 [768, 6144], P(('gy', 'gx'), 'gz')
- w_in_grad: bfloat16 [6144, 24576], P('gz', ('gx', 'gy'))
- w_out_grad: bfloat16 [24576, 6144], P('gx', ('gz', 'gy'))
- bias_grad: float32 [24576], P('gx')
- gain_grad: float32 [6144], P('gz')
The draws below stay inside these ranges and needn't reach their ends.
All inputs are finite; a program needn't handle non-finite values.
Results may differ from the reference program's by a relative error of at most 0.02.
Values may be sent and summed in bfloat16 or wider, within the bound.
A program may use at most 64 MiB of HBM per device.

```python
import jax
import jax.numpy as jnp
from jax import lax

D = 6144
FF = 24576
TOKENS = 768
N_GY = 4
N_GZ = 8


def levels(stream_key, shape, cuts, low, largest):
    def one(position, blocks):
        heights = jax.random.uniform(jax.random.fold_in(jax.random.fold_in(stream_key, 6), position), (blocks,), jnp.float32, low / len(cuts), largest / len(cuts))
        return jnp.repeat(jnp.exp(heights), shape[position] // blocks).reshape((-1,) + (1,) * (len(shape) - position - 1))

    loudness = one(*cuts[0])
    for cut in cuts[1:]:
        loudness = loudness * one(*cut)
    return loudness


def noise(key, shape, deviation, most, cuts=(), dtype=jnp.bfloat16):
    factor_of = levels(key, shape, cuts, -0.22, 0.18) if cuts else 1.0
    array = jax.random.normal(key, shape, jnp.float32) * deviation * factor_of
    return jnp.minimum(jnp.maximum(array, -most), most).astype(dtype)


def setup_inputs(seed: int = 0) -> dict:
    key_list = jax.random.split(jax.random.key(seed), 7)
    tokens = noise(key_list[0], (TOKENS, D), 1.0, 6.0, ((0, 32), (1, 8)))
    gain = jnp.clip(0.5 + 1.0 * jax.random.uniform(key_list[1], (D,), jnp.float32) ** levels(key_list[1], (D,), ((0, 8),), -0.2, 0.2), 0.5, 1.5)
    w_in = noise(key_list[2], (D, FF), D ** -0.5, 0.078125, ((0, 8), (1, 32)))
    b_in = noise(key_list[3], (FF,), 1.0, 4.0, ((0, 8),), jnp.float32)
    w_out = noise(key_list[4], (FF, D), FF ** -0.5, 0.0390625, ((0, 8), (1, 32)))
    cotangent = noise(key_list[5], (TOKENS, D), 1.0, 6.0, ((0, 32), (1, 8)))
    return dict(tokens=tokens, gain=gain, w_in=w_in, b_in=b_in, w_out=w_out, cotangent=cotangent)


epsilon = 1e-06

def split_sum(left_side, right_side, blocks):
    row_count = left_side.shape[0]
    inner = left_side.shape[1] // blocks
    left_blocks = left_side.reshape(row_count, blocks, inner).transpose(1, 0, 2)
    right_blocks = right_side.reshape(blocks, inner, right_side.shape[1])

    def block_step(carry, pieces):
        product = jnp.dot(pieces[0], pieces[1], preferred_element_type=jnp.float32)
        product = lax.optimization_barrier(product.astype(jnp.bfloat16)).astype(jnp.float32)
        return (carry + product, None)
    initial = jnp.zeros((row_count, right_side.shape[1]), jnp.float32)
    summed, _ = lax.scan(block_step, initial, (left_blocks, right_blocks))
    return summed

def reference(tokens, gain, w_in, b_in, w_out, cotangent):
    floats = tokens.astype(jnp.float32)
    row_mean = lax.optimization_barrier(jnp.mean(floats, 1, keepdims=True))
    row_var = lax.optimization_barrier(jnp.mean(floats * floats, 1, keepdims=True)) - row_mean * row_mean
    inv_std = lax.rsqrt(row_var + epsilon)
    centred = (floats - row_mean) * inv_std
    normed = (centred * gain).astype(jnp.bfloat16)
    pre = split_sum(normed, w_in, N_GZ) + b_in
    activated, gelu_back = jax.vjp(jax.nn.gelu, pre)
    activated = activated.astype(jnp.bfloat16)
    y_branch = jnp.dot(activated, w_out, preferred_element_type=jnp.float32).astype(jnp.bfloat16)
    act_grad = split_sum(cotangent, w_out.T, N_GZ)
    pre_grad = gelu_back(act_grad)[0].astype(jnp.bfloat16)
    bias_grad = lax.optimization_barrier(jnp.sum(pre_grad.astype(jnp.float32), 0))
    w_out_grad = split_sum(activated.T, cotangent, N_GY).astype(jnp.bfloat16)
    norm_grad = jnp.dot(pre_grad, w_in.T, preferred_element_type=jnp.float32)
    w_in_grad = split_sum(normed.T, pre_grad, N_GY).astype(jnp.bfloat16)
    hat_grad = norm_grad * gain
    first_mean = lax.optimization_barrier(jnp.mean(hat_grad, 1, keepdims=True))
    second_mean = lax.optimization_barrier(jnp.mean(hat_grad * centred, 1, keepdims=True))
    input_grad = ((hat_grad - first_mean - centred * second_mean) * inv_std).astype(jnp.bfloat16)
    gain_grad = lax.optimization_barrier(jnp.sum(norm_grad * centred, 0))
    return (y_branch, input_grad, w_in_grad, w_out_grad, bias_grad, gain_grad)
```

```python
import jax
import jax.numpy as jnp
from jax import lax
from jax.sharding import PartitionSpec as P

epsilon = 1e-06


def contract_last(left_side, right_side):
    return lax.dot_general(
        left_side, right_side, (((1,), (1,)), ((), ())), preferred_element_type=jnp.float32
    )


def contract_first(left_side, right_side):
    return lax.dot_general(
        left_side, right_side, (((0,), (0,)), ((), ())), preferred_element_type=jnp.float32
    )


def shards(tokens, gain, w_in, b_in, w_out, cotangent):
    floats = tokens.astype(jnp.float32)
    row_sums, row_squares = lax.psum((jnp.sum(floats, 1), jnp.sum(floats * floats, 1)), "gz")
    feature_count = floats.shape[1] * lax.axis_size("gz")
    row_mean = (row_sums / feature_count)[:, None]
    row_var = (row_squares / feature_count)[:, None] - row_mean * row_mean
    inv_std = lax.rsqrt(row_var + epsilon)
    centred = (floats - row_mean) * inv_std
    normed = (centred * gain).astype(jnp.bfloat16)
    normed_all = lax.all_gather(normed, ("gy", "gx"), axis=0, tiled=True)
    grad_all = lax.all_gather(cotangent, ("gy", "gx"), axis=0, tiled=True)
    w_out_use = lax.all_to_all(w_out, "gy", split_axis=0, concat_axis=1, tiled=True)
    hidden = w_in.shape[1]
    bias = lax.dynamic_slice_in_dim(b_in, lax.axis_index("gy") * hidden, hidden)
    pre = (
        lax.psum_scatter(
            jnp.dot(normed_all, w_in, preferred_element_type=jnp.float32).astype(jnp.bfloat16),
            "gz",
            scatter_dimension=0,
            tiled=True,
        ).astype(jnp.float32)
        + bias
    )
    activated, gelu_back = jax.vjp(jax.nn.gelu, pre)
    activated = activated.astype(jnp.bfloat16)
    act_all = lax.all_gather(activated, "gz", axis=0, tiled=True)
    act_grad = lax.psum_scatter(
        contract_last(grad_all, w_out_use).astype(jnp.bfloat16),
        "gz",
        scatter_dimension=0,
        tiled=True,
    ).astype(jnp.float32)
    pre_grad = gelu_back(act_grad)[0].astype(jnp.bfloat16)
    pre_grad_all = lax.all_gather(pre_grad, "gz", axis=0, tiled=True)
    w_out_grad = lax.all_to_all(
        contract_first(act_all, grad_all).astype(jnp.bfloat16),
        "gy",
        split_axis=1,
        concat_axis=0,
        tiled=True,
    )
    y_branch = lax.psum_scatter(
        jnp.dot(act_all, w_out_use, preferred_element_type=jnp.float32).astype(jnp.bfloat16),
        ("gy", "gx"),
        scatter_dimension=0,
        tiled=True,
    )
    norm_grad = lax.psum_scatter(
        contract_last(pre_grad_all, w_in).astype(jnp.bfloat16),
        ("gy", "gx"),
        scatter_dimension=0,
        tiled=True,
    ).astype(jnp.float32)
    w_in_grad = contract_first(normed_all, pre_grad_all).astype(jnp.bfloat16)
    bias_term = jnp.sum(pre_grad_all.astype(jnp.float32), 0)
    bias_grad = lax.all_gather(bias_term, "gy", axis=0, tiled=True)
    hat_grad = norm_grad * gain
    first_sum, second_sum = lax.psum((jnp.sum(hat_grad, 1), jnp.sum(hat_grad * centred, 1)), "gz")
    first_mean = (first_sum / feature_count)[:, None]
    second_mean = (second_sum / feature_count)[:, None]
    input_grad = ((hat_grad - first_mean - centred * second_mean) * inv_std).astype(jnp.bfloat16)
    gain_grad = lax.psum(jnp.sum(norm_grad * centred, 0), ("gx", "gy"))
    return (y_branch, input_grad, w_in_grad, w_out_grad, bias_grad, gain_grad)


def solution(mesh):
    placed = (
        P(("gy", "gx"), "gz"),
        P("gz"),
        P("gz", ("gx", "gy")),
        P("gx"),
        P("gx", ("gz", "gy")),
        P(("gy", "gx"), "gz"),
    )
    return jax.shard_map(
        shards,
        mesh=mesh,
        in_specs=placed,
        out_specs=(
            P(("gy", "gx"), "gz"),
            P(("gy", "gx"), "gz"),
            P("gz", ("gx", "gy")),
            P("gx", ("gz", "gy")),
            P("gx"),
            P("gz"),
        ),
        check_vma=False,
    )
```

```python
import functools

import jax
import jax.numpy as jnp
from jax import lax
from jax.experimental import pallas as pl
from jax.experimental.pallas import tpu as pltpu
from jax.sharding import PartitionSpec as P

epsilon = 1e-06
MESH = pl.DeviceIdType.MESH
BF = jnp.bfloat16
F32 = jnp.float32
NZ = 8
NX = 4
W = 768
CH = 192
HALF = CH // 2
SH = 24
FB = 192
TILE = 256
LANES = 128
COPIES = 140
FEATURES = W * NZ
ROOT = 0.7978845608028654
CUBIC = 0.044715


class Net:
    def __init__(self, send_sems, recv_sems):
        self.send_sems, self.recv_sems = send_sems, recv_sems
        self.count = 0
        self.sent = []

    def send(self, src, dst, **where):
        copy = pltpu.make_async_remote_copy(
            src_ref=src,
            dst_ref=dst,
            send_sem=self.send_sems.at[self.count],
            recv_sem=self.recv_sems.at[self.count],
            device_id=where,
            device_id_type=MESH,
        )
        self.count += 1
        copy.start()
        self.sent.append(copy)
        return copy

    def drain(self):
        for copy in self.sent:
            copy.wait_send()


def dot(left, right, left_dim, right_dim):
    return lax.dot_general(
        left, right, (((left_dim,), (right_dim,)), ((), ())), preferred_element_type=F32
    )


def rows_of(chunk):
    return pl.ds(pl.multiple_of(chunk * CH, CH), CH)


def tiles(body, count=W // TILE, size=TILE):
    def step(i, carry):
        body(pl.ds(pl.multiple_of(i * size, size), size))
        return carry

    lax.fori_loop(0, count, step, 0)


def kernel(
    tok, gain, w_in, b_in, w_out, cot,
    y_out, in_grad, w_in_grad, w_out_grad, b_grad, g_grad,
    g_cot, g_nor, cot_all, nor_all, act_all, pg_all, w_blk, w_full, w_send,
    stat_in, far, side_f, side_b, own, relay, inbox, yx_out, yx_in, pre,
    keep, core_out, core_in, z_out, z_in, total, ty_out, ty_in,
    stat2_in, gz_in, gy_in,
    send_sems, recv_sems,
):
    z, g, q = lax.axis_index("gx"), lax.axis_index("gy"), lax.axis_index("gz")
    yl, c = lax.div(g, 2), lax.rem(g, 2)
    x, h = lax.div(q, 2), lax.rem(q, 2)
    net = Net(send_sems, recv_sems)

    def ring(value, step, size):
        return lax.rem(value + (step + size), size)

    def z_at(step):
        return ring(z, step, NZ)

    def q_at(step):
        return ring(q, step, NZ)

    def g_at(step):
        return ring(g, step, 4)

    def x_at(step):
        return ring(x, step, NX)

    def x_dev(step):
        return x_at(step) * 2 + h

    y_peer = (1 - yl) * 2 + c
    core_peer = yl * 2 + (1 - c)
    h_peer = x * 2 + (1 - h)

    barrier = pltpu.get_barrier_semaphore()
    for s in range(1, NZ):
        pl.semaphore_signal(barrier, inc=1, device_id={"gx": z_at(s)}, device_id_type=MESH)
        pl.semaphore_signal(barrier, inc=1, device_id={"gz": q_at(s)}, device_id_type=MESH)
    for s in range(1, 4):
        pl.semaphore_signal(barrier, inc=1, device_id={"gy": g_at(s)}, device_id_type=MESH)
    pl.semaphore_wait(barrier, 2 * (NZ - 1) + 3)

    turned = [
        net.send(
            w_out.at[pl.ds(pl.multiple_of(g_at(s) * W, W), W)], w_blk.at[g], gy=g_at(s)
        )
        for s in range(1, 4)
    ]
    g_cot[c, z, yl] = cot[...]
    cot_y = net.send(g_cot.at[c, z, yl], g_cot.at[c, z, yl], gy=y_peer)

    lane = lax.broadcasted_iota(jnp.int32, (SH, LANES), 1)

    def pair_tile(first, second):
        return jnp.where(lane < LANES // 2, first, second)

    def split_pair(both):
        return both[:, 0:1], both[:, LANES // 2 : LANES // 2 + 1]

    floats = tok[...].astype(F32)
    stat_in[0] = pair_tile(
        jnp.sum(floats, 1, keepdims=True), jnp.sum(floats * floats, 1, keepdims=True)
    )
    stats = [net.send(stat_in.at[0], stat_in.at[s], gz=q_at(s)) for s in range(1, NZ)]

    class Gather:
        def __init__(self, buf, first):
            self.buf, self.first = buf, first
            self.right, self.left, self.cores = {}, {}, []

        def block(self, step):
            return self.buf.at[c, z_at(step)]

        def forward(self, step, right, left):
            block = self.block(step)
            if right:
                self.right[1 - step] = net.send(block, block, gx=z_at(1))
            if left:
                self.left[1 + step] = net.send(block, block, gx=z_at(-1))
            self.cores.append(net.send(block, block, gy=core_peer))

        def begin(self):
            self.first.wait_recv()
            self.forward(0, True, True)

        def from_left(self, n):
            self.right[n].wait_recv()
            self.forward(-n, n < 4, False)

        def from_right(self, n):
            self.left[n].wait_recv()
            self.forward(n, False, n < 3)

        def finish(self, whole):
            for copy in self.cores:
                copy.wait_recv()
            for block in range(4):
                piece = self.buf[block % 2, :, block // 2].astype(F32).reshape(CH, W)
                whole[pl.ds(block * CH, CH), :] = piece.astype(BF)

    cots = Gather(g_cot, cot_y)
    cots.begin()

    for copy in stats:
        copy.wait_recv()
    both = stat_in[0]
    for s in range(1, NZ):
        both = both + stat_in[s]
    row_sum, row_square = split_pair(both)
    row_mean = row_sum / FEATURES
    row_var = row_square / FEATURES - row_mean * row_mean
    inv_std = lax.rsqrt(row_var + epsilon)

    def centre():
        return (tok[...].astype(F32) - row_mean) * inv_std

    g_nor[c, z, yl] = (centre() * gain[...]).astype(BF)
    nors = Gather(g_nor, net.send(g_nor.at[c, z, yl], g_nor.at[c, z, yl], gy=y_peer))

    cots.from_left(1)
    cots.from_right(1)
    nors.begin()
    cots.from_left(2)
    cots.from_right(2)
    nors.from_left(1)
    nors.from_right(1)
    cots.from_left(3)
    cots.from_right(3)
    nors.from_left(2)
    nors.from_right(2)
    cots.from_left(4)
    nors.from_left(3)
    nors.from_right(3)
    nors.from_left(4)
    nors.finish(nor_all)

    class HiddenSum:
        def __init__(self, n, product):
            self.n, self.product = n, product

        def begin(self):
            n = self.n

            def far_tile(cols):
                far[n, :, cols] = self.product(x_at(2), cols).astype(BF)

            tiles(far_tile)
            self.relays = [
                net.send(far.at[n, pl.ds(0, HALF)], relay.at[n, 0], gz=x_dev(1)),
                net.send(far.at[n, pl.ds(HALF, HALF)], relay.at[n, 1], gz=x_dev(-1)),
            ]
            self.raw = []
            for side, step in enumerate((1, -1)):

                def side_tile(cols):
                    value = self.product(x_at(step), cols)
                    side_f[n, side, :, cols] = value[side * HALF : (side + 1) * HALF]
                    other = 1 - side
                    side_b[n, side, pl.ds(other * HALF, HALF), cols] = value[
                        other * HALF : (other + 1) * HALF
                    ].astype(BF)

                tiles(side_tile)
                part = pl.ds((1 - side) * HALF, HALF)
                self.raw.append(
                    net.send(side_b.at[n, side, part], inbox.at[n, side, part], gz=x_dev(step))
                )

            def own_tile(cols):
                own[n, :, cols] = self.product(x, cols)

            tiles(own_tile)

        def relayed(self):
            n = self.n
            self.summed = []
            for side, step in enumerate((1, -1)):
                self.relays[side].wait_recv()
                part = pl.ds(side * HALF, HALF)

                def add_tile(cols):
                    value = side_f[n, side, :, cols] + relay[n, side, :, cols].astype(F32)
                    side_b[n, side, part, cols] = value.astype(BF)

                tiles(add_tile)
                self.summed.append(
                    net.send(side_b.at[n, side, part], inbox.at[n, side, part], gz=x_dev(step))
                )

        def pair_up(self):
            n = self.n
            self.pairs = []
            for part_index in range(2):
                part = pl.ds(part_index * HALF, HALF)
                self.summed[part_index].wait_recv()
                self.raw[1 - part_index].wait_recv()

                def add_tile(cols):
                    value = own[n, part, cols] + inbox[n, 0, part, cols].astype(F32)
                    value = value + inbox[n, 1, part, cols].astype(F32)
                    yx_out[n, part, cols] = value.astype(BF)

                tiles(add_tile)
                self.pairs.append(
                    net.send(yx_out.at[n, part], yx_in.at[n, part], gz=h_peer)
                )

        def total(self, rows):
            n = self.n
            return yx_out[n, rows, :].astype(F32) + yx_in[n, rows, :].astype(F32)

    pres = HiddenSum(0, lambda k, cols: dot(nor_all[rows_of(k), :], w_in[:, cols], 1, 0))
    grads = HiddenSum(1, lambda k, cols: dot(cot_all[rows_of(k), :], w_full[cols, :], 1, 1))

    pres.begin()

    cots.finish(cot_all)
    w_blk[g] = w_out[pl.ds(pl.multiple_of(g * W, W), W), :]
    for copy in turned:
        copy.wait_recv()

    def assemble(rows):
        w_full[rows, :] = jnp.concatenate([w_blk[i, rows, :] for i in range(4)], axis=1)

    tiles(assemble)

    pres.relayed()
    grads.begin()
    pres.pair_up()
    grads.relayed()

    bias = b_in[:, pl.ds(pl.multiple_of(g * W, W), W)]
    mine = pl.multiple_of(x * CH, CH)

    class HiddenGather:
        def __init__(self, whole):
            self.whole = whole
            rows = whole.at[pl.ds(mine, CH)]
            self.sides = [net.send(rows, rows, gz=x_dev(step)) for step in (1, -1)]

        def onward(self):
            self.onwards = []
            for side, step in enumerate((1, -1)):
                self.sides[side].wait_recv()
                start = pl.multiple_of(x_at(-step) * CH + side * HALF, HALF)
                rows = self.whole.at[pl.ds(start, HALF)]
                self.onwards.append(net.send(rows, rows, gz=x_dev(step)))

        def finish(self):
            for copy in self.onwards:
                copy.wait_recv()

    STEP = 32
    for part_index in range(2):
        pres.pairs[part_index].wait_recv()

        def activate(i, carry):
            start = pl.multiple_of(part_index * HALF + i * STEP, STEP)
            rows = pl.ds(start, STEP)
            v = pres.total(rows) + bias
            t = jnp.tanh(ROOT * (v + CUBIC * v * v * v))
            act_all[pl.ds(pl.multiple_of(mine + start, STEP), STEP), :] = (
                0.5 * v * (1.0 + t)
            ).astype(BF)
            pre[rows, :] = 0.5 * (1.0 + t) + 0.5 * v * (1.0 - t * t) * ROOT * (
                1.0 + 3.0 * CUBIC * v * v
            )
            return carry

        lax.fori_loop(0, HALF // STEP, activate, 0)
    acts = HiddenGather(act_all)

    grads.pair_up()
    acts.onward()
    for part_index in range(2):
        grads.pairs[part_index].wait_recv()

        def backward(i, carry):
            start = pl.multiple_of(part_index * HALF + i * STEP, STEP)
            rows = pl.ds(start, STEP)
            pg_all[pl.ds(pl.multiple_of(mine + start, STEP), STEP), :] = (
                grads.total(rows) * pre[rows, :]
            ).astype(BF)
            return carry

        lax.fori_loop(0, HALF // STEP, backward, 0)
    pgs = HiddenGather(pg_all)

    class FeatureSum:
        def __init__(self, n, product):
            self.n, self.product = n, product
            self.cores, self.spread = {}, {}

        def products(self, order):
            n = self.n
            j = lax.div(x, 2) if order == 0 else 1 - lax.div(x, 2)

            def send_tile(cols):
                value = self.product(2 * j + (1 - c), cols)
                core_out[n, order, :, :, cols] = value.reshape(NZ, SH, TILE).astype(BF)

            tiles(send_tile)
            self.cores[order] = net.send(
                core_out.at[n, order], core_in.at[n, order], gy=core_peer
            )

            def keep_tile(cols):
                value = self.product(2 * j + c, cols)
                keep[n, order, :, :, cols] = value.reshape(NZ, SH, TILE)

            tiles(keep_tile)

        def scatter(self, order):
            n = self.n
            self.cores[order].wait_recv()

            def add_one(i, carry):
                value = keep[n, order, i] + core_in[n, order, i].astype(F32)
                keep[n, order, i] = value
                z_out[n, order, i] = value.astype(BF)
                return carry

            lax.fori_loop(0, NZ, add_one, 0)
            self.spread[order] = [
                net.send(z_out.at[n, order, z_at(s)], z_in.at[n, order, s - 1], gx=z_at(s))
                for s in range(1, NZ)
            ]

        def collect(self, order):
            n = self.n
            for copy in self.spread[order]:
                copy.wait_recv()
            value = keep[n, order, z]
            for s in range(NZ - 1):
                value = value + z_in[n, order, s].astype(F32)
            total[n, order] = value

        def exchange(self):
            n = self.n
            here = lax.rem(lax.div(x, 2) + yl, 2)
            ty_out[n] = total[n, 1 - here].astype(BF)
            self.last = net.send(ty_out.at[n], ty_in.at[n], gy=y_peer)
            self.here = here

        def result(self):
            self.last.wait_recv()
            return total[self.n, self.here] + ty_in[self.n].astype(F32)

    ys = FeatureSum(0, lambda k, cols: dot(act_all[rows_of(k), :], w_full[:, cols], 1, 0))
    norms = FeatureSum(1, lambda k, cols: dot(pg_all[rows_of(k), :], w_in[cols, :], 1, 1))

    ys.products(0)
    ys.scatter(0)
    acts.finish()
    ys.products(1)
    ys.scatter(1)

    def w_out_tile(rows):
        value = dot(act_all[:, rows], cot_all[...], 0, 0)
        for i in range(4):
            w_send[i, rows, :] = value[:, i * FB : (i + 1) * FB].astype(BF)

    tiles(w_out_tile)
    own_rows = pl.ds(pl.multiple_of(g * W, W), W)
    returned = [
        net.send(w_send.at[g_at(s)], w_out_grad.at[own_rows], gy=g_at(s)) for s in range(1, 4)
    ]
    w_out_grad[own_rows, :] = w_send[g]

    pgs.onward()
    ys.collect(0)
    norms.products(0)
    norms.scatter(0)
    ys.collect(1)
    ys.exchange()
    pgs.finish()
    norms.products(1)
    norms.scatter(1)

    def bias_sum(i, carry):
        rows = pl.ds(pl.multiple_of(i * STEP, STEP), STEP)
        return carry + jnp.sum(pg_all[rows, :].astype(F32), 0, keepdims=True)

    b_grad[g] = lax.fori_loop(0, W // STEP, bias_sum, jnp.zeros((1, W), F32))
    biases = [net.send(b_grad.at[g], b_grad.at[g], gy=g_at(s)) for s in range(1, 4)]

    def w_in_tile(rows):
        w_in_grad[rows, :] = dot(nor_all[:, rows], pg_all[...], 0, 0).astype(BF)

    tiles(w_in_tile)

    norms.collect(0)
    norms.collect(1)
    norms.exchange()
    y_out[...] = ys.result().astype(BF)

    norm_grad = norms.result()
    centred = centre()
    hat_grad = norm_grad * gain[...]
    stat2_in[0] = pair_tile(
        jnp.sum(hat_grad, 1, keepdims=True), jnp.sum(hat_grad * centred, 1, keepdims=True)
    )
    stats2 = [net.send(stat2_in.at[0], stat2_in.at[s], gz=q_at(s)) for s in range(1, NZ)]
    gz_in[z] = jnp.sum(norm_grad * centred, 0, keepdims=True)
    gains = [net.send(gz_in.at[z], gz_in.at[z], gx=z_at(s)) for s in range(1, NZ)]
    for copy in gains:
        copy.wait_recv()
    value = gz_in[0]
    for i in range(1, NZ):
        value = value + gz_in[i]
    gy_in[g] = value
    gains = [net.send(gy_in.at[g], gy_in.at[g], gy=g_at(s)) for s in range(1, 4)]
    for copy in stats2:
        copy.wait_recv()
    both = stat2_in[0]
    for s in range(1, NZ):
        both = both + stat2_in[s]
    first, second = split_pair(both)
    in_grad[...] = (
        (hat_grad - first / FEATURES - centred * (second / FEATURES)) * inv_std
    ).astype(BF)
    for copy in gains:
        copy.wait_recv()
    g_grad[...] = (gy_in[0] + gy_in[1]) + (gy_in[2] + gy_in[3])
    for copy in biases + returned:
        copy.wait_recv()
    net.drain()


def shards(tokens, gain, w_in, b_in, w_out, cotangent):
    vmem = pl.BlockSpec(memory_space=pltpu.VMEM)
    outs = pl.pallas_call(
        kernel,
        out_shape=(
            jax.ShapeDtypeStruct((SH, W), BF),
            jax.ShapeDtypeStruct((SH, W), BF),
            jax.ShapeDtypeStruct((W, W), BF),
            jax.ShapeDtypeStruct((4 * W, FB), BF),
            jax.ShapeDtypeStruct((4, 1, W), F32),
            jax.ShapeDtypeStruct((1, W), F32),
        ),
        in_specs=[vmem] * 6,
        out_specs=[vmem] * 6,
        scratch_shapes=[
            pltpu.VMEM((2, NZ, 2, SH, W), BF),
            pltpu.VMEM((2, NZ, 2, SH, W), BF),
            pltpu.VMEM((W, W), BF),
            pltpu.VMEM((W, W), BF),
            pltpu.VMEM((W, W), BF),
            pltpu.VMEM((W, W), BF),
            pltpu.VMEM((4, W, FB), BF),
            pltpu.VMEM((W, W), BF),
            pltpu.VMEM((4, W, FB), BF),
            pltpu.VMEM((NZ, SH, LANES), F32),
            pltpu.VMEM((2, CH, W), BF),
            pltpu.VMEM((2, 2, HALF, W), F32),
            pltpu.VMEM((2, 2, CH, W), BF),
            pltpu.VMEM((2, CH, W), F32),
            pltpu.VMEM((2, 2, HALF, W), BF),
            pltpu.VMEM((2, 2, CH, W), BF),
            pltpu.VMEM((2, CH, W), BF),
            pltpu.VMEM((2, CH, W), BF),
            pltpu.VMEM((CH, W), F32),
            pltpu.VMEM((2, 2, NZ, SH, W), F32),
            pltpu.VMEM((2, 2, NZ, SH, W), BF),
            pltpu.VMEM((2, 2, NZ, SH, W), BF),
            pltpu.VMEM((2, 2, NZ, SH, W), BF),
            pltpu.VMEM((2, 2, NZ, SH, W), BF),
            pltpu.VMEM((2, 2, SH, W), F32),
            pltpu.VMEM((2, SH, W), BF),
            pltpu.VMEM((2, SH, W), BF),
            pltpu.VMEM((NZ, SH, LANES), F32),
            pltpu.VMEM((NZ, 1, W), F32),
            pltpu.VMEM((4, 1, W), F32),
            pltpu.SemaphoreType.DMA((COPIES,)),
            pltpu.SemaphoreType.DMA((COPIES,)),
        ],
        compiler_params=pltpu.CompilerParams(
            collective_id=0, has_side_effects=True, vmem_limit_bytes=58 << 20
        ),
        cost_estimate=pl.CostEstimate(
            flops=12 * W * W * W, bytes_accessed=10 * W * W, transcendentals=CH * W
        ),
    )(tokens, gain.reshape(1, W), w_in, b_in.reshape(1, 4 * W), w_out, cotangent)
    y_branch, input_grad, w_in_grad, w_out_grad, bias_grad, gain_grad = outs
    return (
        y_branch,
        input_grad,
        w_in_grad,
        w_out_grad,
        bias_grad.reshape(4 * W),
        gain_grad.reshape(W),
    )


def solution(mesh):
    placed = (
        P(("gy", "gx"), "gz"),
        P("gz"),
        P("gz", ("gx", "gy")),
        P("gx"),
        P("gx", ("gz", "gy")),
        P(("gy", "gx"), "gz"),
    )
    return jax.shard_map(
        shards,
        mesh=mesh,
        in_specs=placed,
        out_specs=(
            P(("gy", "gx"), "gz"),
            P(("gy", "gx"), "gz"),
            P("gz", ("gx", "gy")),
            P("gx", ("gz", "gy")),
            P("gx"),
            P("gz"),
        ),
        check_vma=False,
    )
```

```python
import functools

import jax
import jax.numpy as jnp
from jax import lax
from jax.experimental import pallas as pl
from jax.experimental.pallas import tpu as pltpu
from jax.sharding import PartitionSpec as P

epsilon = 1e-06
MESH = pl.DeviceIdType.MESH
BF = jnp.bfloat16
F32 = jnp.float32
NZ = 8
NX = 4
W = 768
CH = 192
HALF = CH // 2
SH = 24
FB = 192
TILE = 256
LANES = 128
PARTS = (slice(0, W // 2), slice(W // 2, W))
COPIES = 170
FEATURES = W * NZ
ROOT = 0.7978845608028654
CUBIC = 0.044715


class Sent:
    def __init__(self, copy):
        self.copy, self.waited = copy, False

    def wait_recv(self):
        if not self.waited:
            self.waited = True
            self.copy.wait_recv()


class Local:
    def __init__(self, copy):
        self.copy, self.waited = copy, False

    def wait(self):
        if not self.waited:
            self.waited = True
            self.copy.wait()


class Net:
    def __init__(self, send_sems, recv_sems, local_sems):
        self.local_sems, self.locals = local_sems, []
        self.send_sems, self.recv_sems = send_sems, recv_sems
        self.count = 0
        self.sent = []

    def send(self, src, dst, **where):
        copy = pltpu.make_async_remote_copy(
            src_ref=src,
            dst_ref=dst,
            send_sem=self.send_sems.at[self.count],
            recv_sem=self.recv_sems.at[self.count],
            device_id=where,
            device_id_type=MESH,
        )
        self.count += 1
        copy.start()
        self.sent.append(Sent(copy))
        return self.sent[-1]

    def local(self, src, dst):
        copy = pltpu.make_async_copy(src, dst, self.local_sems.at[len(self.locals)])
        copy.start()
        self.locals.append(Local(copy))
        return self.locals[-1]

    def drain(self):
        for copy in self.locals:
            copy.wait()
        for sent in self.sent:
            sent.wait_recv()
            sent.copy.wait_send()


def dot(left, right, left_dim, right_dim):
    return lax.dot_general(
        left, right, (((left_dim,), (right_dim,)), ((), ())), preferred_element_type=F32
    )


def rows_of(chunk):
    return pl.ds(pl.multiple_of(chunk * CH, CH), CH)


def tiles(body, count=W // TILE, size=TILE):
    def step(i, carry):
        body(pl.ds(pl.multiple_of(i * size, size), size))
        return carry

    lax.fori_loop(0, count, step, 0)


def kernel(
    tok, gain, w_in_hbm, b_in, w_out, cot,
    y_out, in_grad, w_in_grad, w_out_grad, b_grad, g_grad,
    g_cot, g_tok, cot_all, nor_all, act_all, pg_all, w_in, w_full, w_send, w_in_out,
    stat_in, stat_all, far, side_f, side_b, own, relay, inbox, yx_out, yx_in, pre,
    keep, core_out, core_in, z_out, z_in, z_three, z_four, z_two, total, ty_out, ty_in,
    stat2_in, gz_in, gy_in,
    send_sems, recv_sems, local_sems,
):
    z, g, q = lax.axis_index("gx"), lax.axis_index("gy"), lax.axis_index("gz")
    yl, c = lax.div(g, 2), lax.rem(g, 2)
    x, h = lax.div(q, 2), lax.rem(q, 2)
    net = Net(send_sems, recv_sems, local_sems)

    def ring(value, step, size):
        return lax.rem(value + (step + size), size)

    def z_at(step):
        return ring(z, step, NZ)

    def q_at(step):
        return ring(q, step, NZ)

    def g_at(step):
        return ring(g, step, 4)

    def x_at(step):
        return ring(x, step, NX)

    def x_dev(step):
        return x_at(step) * 2 + h

    y_peer = (1 - yl) * 2 + c
    core_peer = yl * 2 + (1 - c)
    h_peer = x * 2 + (1 - h)

    def hidden_of(group):
        return pl.ds(pl.multiple_of(group * W, W), W)

    def features_of(group):
        return pl.ds(pl.multiple_of(group * FB, FB), FB)

    load_w_in = net.local(w_in_hbm, w_in)
    load_w_out = net.local(w_out.at[:, hidden_of(g)], w_full.at[features_of(g)])

    barrier = pltpu.get_barrier_semaphore()
    for s in range(1, NZ):
        pl.semaphore_signal(barrier, inc=1, device_id={"gx": z_at(s)}, device_id_type=MESH)
        pl.semaphore_signal(barrier, inc=1, device_id={"gz": q_at(s)}, device_id_type=MESH)
    for s in range(1, 4):
        pl.semaphore_signal(barrier, inc=1, device_id={"gy": g_at(s)}, device_id_type=MESH)

    lane = lax.broadcasted_iota(jnp.int32, (SH, LANES), 1)
    row = lax.broadcasted_iota(jnp.int32, (SH, LANES), 0)
    MID = LANES // 2

    def pair_tile(first, second):
        return jnp.where(lane < MID, first, second)

    def split_pair(both):
        return both[:, 0:1], both[:, MID : MID + 1]

    floats = tok[...].astype(F32)
    stat_in[0] = pair_tile(
        jnp.sum(floats, 1, keepdims=True), jnp.sum(floats * floats, 1, keepdims=True)
    )
    g_tok[c, z, yl] = tok[...]
    g_cot[c, z, yl] = cot[...]
    pl.semaphore_wait(barrier, 2 * (NZ - 1) + 3)

    stats = [net.send(stat_in.at[0], stat_in.at[s], gz=q_at(s)) for s in range(1, NZ)]

    class Lane:
        def __init__(self, which):
            self.which, self.right, self.left = which, {}, {}
            self.forward(0, True, True)

        def forward(self, step, right, left):
            block = g_tok.at[c, z_at(step), self.which]
            if right:
                self.right[1 - step] = net.send(block, block, gx=z_at(1))
            if left:
                self.left[1 + step] = net.send(block, block, gx=z_at(-1))

        def onward(self, n):
            self.right[n].wait_recv()
            self.forward(-n, n < 4, False)
            if n < 4:
                self.left[n].wait_recv()
                self.forward(n, False, n < 3)

    def tok_to_core(step):
        block = g_tok.at[c, z_at(step)]
        tok_cores.append(net.send(block, block, gy=core_peer))

    class Gather:
        def __init__(self, buf):
            self.buf = buf
            self.first = net.send(buf.at[c, z, yl], buf.at[c, z, yl], gy=y_peer)
            self.right, self.left, self.cores = {}, {}, []

        def forward(self, step, right, left):
            block = self.buf.at[c, z_at(step)]
            if right:
                self.right[1 - step] = net.send(block, block, gx=z_at(1))
            if left:
                self.left[1 + step] = net.send(block, block, gx=z_at(-1))
            self.cores.append(net.send(block, block, gy=core_peer))

        def begin(self):
            self.first.wait_recv()
            self.forward(0, True, True)

        def onward(self, n):
            self.right[n].wait_recv()
            self.forward(-n, n < 4, False)
            if n < 4:
                self.left[n].wait_recv()
                self.forward(n, False, n < 3)

        def finish(self, whole):
            for copy in self.cores:
                copy.wait_recv()
            for block in range(4):
                piece = self.buf[block % 2, :, block // 2].astype(F32).reshape(CH, W)
                whole[pl.ds(block * CH, CH), :] = piece.astype(BF)

    tok_cores = []
    tok_y = net.send(g_tok.at[c, z, yl], g_tok.at[c, z, yl], gy=y_peer)
    near = Lane(yl)
    cots = Gather(g_cot)
    turned = [
        net.send(w_out.at[:, hidden_of(g_at(s))], w_full.at[features_of(g)], gy=g_at(s))
        for s in range(1, 4)
    ]
    tok_y.wait_recv()
    across = Lane(1 - yl)
    tok_to_core(0)
    near.onward(1)
    cots.begin()
    for copy in stats:
        copy.wait_recv()
    both = stat_in[0]
    for s in range(1, NZ):
        both = both + stat_in[s]
    row_sum, row_square = split_pair(both)
    row_mean = row_sum / FEATURES
    row_var = row_square / FEATURES - row_mean * row_mean
    inv_std = lax.rsqrt(row_var + epsilon)

    def gain_row():
        return gain[...].reshape(1, W)

    def centre():
        return (tok[...].astype(F32) - row_mean) * inv_std

    on_row = lane == row
    on_mid = lane == row + MID

    def rows_centred(target):
        packed = stat_all[2 * target + c, z]
        means = jnp.sum(jnp.where(on_row, packed, 0.0), 1, keepdims=True)
        scales = jnp.sum(jnp.where(on_mid, packed, 0.0), 1, keepdims=True)
        return (g_tok[c, z, target].astype(F32) - means) * scales

    stat_all[g, z] = jnp.sum(
        jnp.where(on_row, row_mean, 0.0) + jnp.where(on_mid, inv_std, 0.0), 0, keepdims=True
    )
    stats = [net.send(stat_all.at[g, z], stat_all.at[g, z], gx=z_at(s)) for s in range(1, NZ)]

    across.onward(1)
    tok_to_core(1)
    tok_to_core(-1)
    near.onward(2)
    for copy in stats:
        copy.wait_recv()
    stats = [net.send(stat_all.at[g], stat_all.at[g], gy=g_at(s)) for s in range(1, 4)]
    across.onward(2)
    tok_to_core(2)
    tok_to_core(-2)
    cots.onward(1)
    near.onward(3)
    across.onward(3)
    tok_to_core(3)
    tok_to_core(-3)
    cots.onward(2)
    near.onward(4)
    across.onward(4)
    tok_to_core(-4)
    for copy in stats:
        copy.wait_recv()
    for copy in tok_cores:
        copy.wait_recv()
    gains_row = gain_row()
    for block in range(4):
        packed = stat_all[block]
        means = jnp.sum(jnp.where(on_row[None], packed, 0.0), 2, keepdims=True)
        scales = jnp.sum(jnp.where(on_mid[None], packed, 0.0), 2, keepdims=True)
        piece = (g_tok[block % 2, :, block // 2].astype(F32) - means) * scales
        nor_all[pl.ds(block * CH, CH), :] = (
            (piece * gains_row[None]).reshape(CH, W).astype(BF)
        )

    class HiddenSum:
        def __init__(self, n, product):
            self.n, self.product = n, product

        def begin(self, between=()):
            n = self.n

            def far_tile(cols):
                far[n, :, cols] = self.product(x_at(2), cols).astype(BF)

            tiles(far_tile)
            self.relays = [
                net.send(far.at[n, pl.ds(0, HALF)], relay.at[n, 0], gz=x_dev(1)),
                net.send(far.at[n, pl.ds(HALF, HALF)], relay.at[n, 1], gz=x_dev(-1)),
            ]
            for action in between:
                action()
            self.raw = []
            for side, step in enumerate((1, -1)):

                def side_tile(cols):
                    value = self.product(x_at(step), cols)
                    side_f[n, side, :, cols] = value[side * HALF : (side + 1) * HALF]
                    other = 1 - side
                    side_b[n, side, pl.ds(other * HALF, HALF), cols] = value[
                        other * HALF : (other + 1) * HALF
                    ].astype(BF)

                tiles(side_tile)
                part = pl.ds((1 - side) * HALF, HALF)
                self.raw.append(
                    net.send(side_b.at[n, side, part], inbox.at[n, side, part], gz=x_dev(step))
                )

            def own_tile(cols):
                own[n, :, cols] = self.product(x, cols)

            tiles(own_tile)

        def relayed(self):
            n = self.n
            self.summed = []
            for side, step in enumerate((1, -1)):
                self.relays[side].wait_recv()
                part = pl.ds(side * HALF, HALF)

                def add_tile(cols):
                    value = side_f[n, side, :, cols] + relay[n, side, :, cols].astype(F32)
                    side_b[n, side, part, cols] = value.astype(BF)

                tiles(add_tile)
                self.summed.append(
                    net.send(side_b.at[n, side, part], inbox.at[n, side, part], gz=x_dev(step))
                )

        def pair_up(self):
            n = self.n
            self.pairs = []
            for part_index in range(2):
                part = pl.ds(part_index * HALF, HALF)
                self.summed[part_index].wait_recv()
                self.raw[1 - part_index].wait_recv()

                def add_tile(cols):
                    value = own[n, part, cols] + inbox[n, 0, part, cols].astype(F32)
                    value = value + inbox[n, 1, part, cols].astype(F32)
                    yx_out[n, part, cols] = value.astype(BF)

                tiles(add_tile)
                self.pairs.append(
                    net.send(yx_out.at[n, part], yx_in.at[n, part], gz=h_peer)
                )

        def total(self, rows):
            n = self.n
            return yx_out[n, rows, :].astype(F32) + yx_in[n, rows, :].astype(F32)

    pres = HiddenSum(0, lambda k, cols: dot(nor_all[rows_of(k), :], w_in[:, cols], 1, 0))
    grads = HiddenSum(1, lambda k, cols: dot(cot_all[rows_of(k), :], w_full[:, cols], 1, 0))

    load_w_in.wait()
    pres.begin([lambda: cots.onward(3)])

    cots.onward(4)
    cots.finish(cot_all)
    for copy in turned:
        copy.wait_recv()
    load_w_out.wait()

    pres.relayed()
    grads.begin()
    pres.pair_up()
    grads.relayed()

    bias = b_in[:, pl.ds(pl.multiple_of(g * W, W), W)]
    mine = pl.multiple_of(x * CH, CH)

    class HiddenGather:
        def __init__(self, whole):
            self.whole = whole
            rows = whole.at[pl.ds(mine, CH)]
            self.sides = [net.send(rows, rows, gz=x_dev(step)) for step in (1, -1)]

        def onward(self):
            self.onwards = []
            for side, step in enumerate((1, -1)):
                self.sides[side].wait_recv()
                start = pl.multiple_of(x_at(-step) * CH + side * HALF, HALF)
                rows = self.whole.at[pl.ds(start, HALF)]
                self.onwards.append(net.send(rows, rows, gz=x_dev(step)))

        def finish(self):
            for copy in self.onwards:
                copy.wait_recv()

    class FeatureSum:
        def __init__(self, n, product):
            self.n, self.product = n, product
            self.cores, self.three, self.four, self.last_hops = {}, {}, {}, {}

        def target(self, order):
            return lax.div(x, 2) if order == 0 else 1 - lax.div(x, 2)

        def products(self, order):
            n, j = self.n, self.target(order)

            def send_tile(cols):
                value = self.product(2 * j + (1 - c), cols)
                core_out[n, order, :, :, cols] = value.reshape(NZ, SH, TILE).astype(BF)

            tiles(send_tile)
            self.cores[order] = net.send(
                core_out.at[n, order], core_in.at[n, order], gy=core_peer
            )

            def keep_tile(cols):
                value = self.product(2 * j + c, cols)
                keep[n, order, :, :, cols] = value.reshape(NZ, SH, TILE)

            tiles(keep_tile)

        def scatter(self, order):
            n = self.n
            self.cores[order].wait_recv()

            def add_one(i, carry):
                value = keep[n, order, i] + core_in[n, order, i].astype(F32)
                keep[n, order, i] = value
                z_out[n, order, i] = value.astype(BF)
                return carry

            lax.fori_loop(0, NZ, add_one, 0)
            out, sides = z_out.at[n, order], tuple(enumerate((1, -1)))
            self.three[order] = [
                net.send(out.at[z_at(3 * d)], z_three.at[n, order, i], gx=z_at(d))
                for i, d in sides
            ]
            self.four[order] = [
                net.send(
                    out.at[z_at(4), :, part], z_four.at[n, order, i, :, part], gx=z_at(2 * d)
                )
                for (i, d), part in zip(sides, PARTS)
            ]
            self.last_hops[order] = [
                net.send(out.at[z_at(d)], z_in.at[n, order, i], gx=z_at(d)) for i, d in sides
            ]

        def relay(self, order):
            n = self.n
            for i, d in enumerate((1, -1)):
                self.three[order][i].wait_recv()
                self.four[order][i].wait_recv()
                dest = z_at(2 * d)
                for k, part in enumerate(PARTS):
                    value = keep[n, order, dest, :, part]
                    value = value + z_three[n, order, i, :, part].astype(F32)
                    if k == i:
                        value = value + z_four[n, order, i, :, part].astype(F32)
                    z_two[n, order, i, :, part] = value.astype(BF)
                self.last_hops[order].append(
                    net.send(z_two.at[n, order, i], z_in.at[n, order, 2 + i], gx=dest)
                )

        def collect(self, order):
            n = self.n
            for copy in self.last_hops[order]:
                copy.wait_recv()
            value = keep[n, order, z]
            for s in range(4):
                value = value + z_in[n, order, s].astype(F32)
            total[n, order] = value

        def exchange(self):
            n = self.n
            here = lax.rem(lax.div(x, 2) + yl, 2)
            ty_out[n] = total[n, 1 - here].astype(BF)
            self.last = net.send(ty_out.at[n], ty_in.at[n], gy=y_peer)
            self.here = here

        def result(self):
            self.last.wait_recv()
            return total[self.n, self.here] + ty_in[self.n].astype(F32)

    ys = FeatureSum(0, lambda k, cols: dot(act_all[rows_of(k), :], w_full[cols, :], 1, 1))
    norms = FeatureSum(1, lambda k, cols: dot(pg_all[rows_of(k), :], w_in[cols, :], 1, 1))

    STEP = 32
    for part_index in range(2):
        pres.pairs[part_index].wait_recv()

        def activate(i, carry):
            start = pl.multiple_of(part_index * HALF + i * STEP, STEP)
            rows = pl.ds(start, STEP)
            v = pres.total(rows) + bias
            t = jnp.tanh(ROOT * (v + CUBIC * v * v * v))
            act_all[pl.ds(pl.multiple_of(mine + start, STEP), STEP), :] = (
                0.5 * v * (1.0 + t)
            ).astype(BF)
            pre[rows, :] = 0.5 * (1.0 + t) + 0.5 * v * (1.0 - t * t) * ROOT * (
                1.0 + 3.0 * CUBIC * v * v
            )
            return carry

        lax.fori_loop(0, HALF // STEP, activate, 0)
    acts = HiddenGather(act_all)

    grads.pair_up()
    acts.onward()
    ys.products(0)
    for part_index in range(2):
        grads.pairs[part_index].wait_recv()

        def backward(i, carry):
            start = pl.multiple_of(part_index * HALF + i * STEP, STEP)
            rows = pl.ds(start, STEP)
            pg_all[pl.ds(pl.multiple_of(mine + start, STEP), STEP), :] = (
                grads.total(rows) * pre[rows, :]
            ).astype(BF)
            return carry

        lax.fori_loop(0, HALF // STEP, backward, 0)
    pgs = HiddenGather(pg_all)

    ys.scatter(0)
    acts.finish()
    ys.products(1)
    ys.relay(0)

    def w_out_tile(rows):
        w_send[rows, :] = dot(cot_all[:, rows], act_all[...], 0, 0).astype(BF)

    tiles(w_out_tile)
    for s in range(1, 4):
        net.send(
            w_send.at[features_of(g_at(s))], w_out_grad.at[:, hidden_of(g)], gy=g_at(s)
        )
    net.local(w_send.at[features_of(g)], w_out_grad.at[:, hidden_of(g)])
    ys.scatter(1)
    pgs.onward()
    norms.products(0)
    ys.relay(1)
    norms.scatter(0)
    ys.collect(0)
    ys.collect(1)
    ys.exchange()
    pgs.finish()
    norms.products(1)
    norms.relay(0)
    norms.scatter(1)

    def bias_sum(i, carry):
        rows = pl.ds(pl.multiple_of(i * STEP, STEP), STEP)
        return carry + jnp.sum(pg_all[rows, :].astype(F32), 0, keepdims=True)

    b_grad[g] = lax.fori_loop(0, W // STEP, bias_sum, jnp.zeros((1, W), F32))
    biases = [net.send(b_grad.at[g], b_grad.at[g], gy=g_at(s)) for s in range(1, 4)]

    def w_in_tile(rows):
        w_in_out[rows, :] = dot(nor_all[:, rows], pg_all[...], 0, 0).astype(BF)

    tiles(w_in_tile)
    net.local(w_in_out, w_in_grad)

    norms.relay(1)
    norms.collect(0)
    norms.collect(1)
    norms.exchange()
    gz_in[z] = sum(
        jnp.sum(total[1, order] * rows_centred(norms.target(order)), 0, keepdims=True)
        for order in range(2)
    )
    gains = [net.send(gz_in.at[z], gz_in.at[z], gx=z_at(s)) for s in range(1, NZ)]
    y_out[...] = ys.result().astype(BF)

    norm_grad = norms.result()
    centred = centre()
    hat_grad = norm_grad * gain_row()
    stat2_in[0] = pair_tile(
        jnp.sum(hat_grad, 1, keepdims=True), jnp.sum(hat_grad * centred, 1, keepdims=True)
    )
    stats2 = [net.send(stat2_in.at[0], stat2_in.at[s], gz=q_at(s)) for s in range(1, NZ)]
    for copy in gains:
        copy.wait_recv()
    value = gz_in[0]
    for i in range(1, NZ):
        value = value + gz_in[i]
    gy_in[g] = value
    gains = [net.send(gy_in.at[g], gy_in.at[g], gy=g_at(s)) for s in range(1, 4)]
    for copy in stats2:
        copy.wait_recv()
    both = stat2_in[0]
    for s in range(1, NZ):
        both = both + stat2_in[s]
    first, second = split_pair(both)
    in_grad[...] = (
        (hat_grad - first / FEATURES - centred * (second / FEATURES)) * inv_std
    ).astype(BF)
    for copy in gains:
        copy.wait_recv()
    g_grad[...] = (gy_in[0] + gy_in[1]) + (gy_in[2] + gy_in[3])
    net.drain()


def hand_over(*refs):
    ins, outs, held, sems = refs[:6], refs[6:12], refs[12:17], refs[17]
    order = (2, 3, 0, 1, 4)
    first = {i: pltpu.make_async_copy(ins[i], held[i], sems.at[i]) for i in order}
    second = {i: pltpu.make_async_copy(held[i], outs[i], sems.at[5 + i]) for i in order}
    for i in order:
        first[i].start()
    outs[5][...] = ins[5][...].reshape(W)
    for i in order:
        first[i].wait()
        second[i].start()
    for i in order:
        second[i].wait()


def shards(tokens, gain, w_in, b_in, w_out, cotangent):
    vmem = pl.BlockSpec(memory_space=pltpu.VMEM)
    hbm = pl.BlockSpec(memory_space=pl.ANY)
    results = (
        jax.ShapeDtypeStruct((SH, W), BF),
        jax.ShapeDtypeStruct((SH, W), BF),
        jax.ShapeDtypeStruct((W, W), BF),
        jax.ShapeDtypeStruct((FB, 4 * W), BF),
        jax.ShapeDtypeStruct((4, 1, W), F32),
        jax.ShapeDtypeStruct((1, W), F32),
    )
    outs = pl.pallas_call(
        kernel,
        out_shape=results,
        in_specs=[vmem, vmem, hbm, vmem, hbm, vmem],
        out_specs=[vmem, vmem, hbm, hbm, vmem, vmem],
        scratch_shapes=[
            pltpu.VMEM((2, NZ, 2, SH, W), BF),
            pltpu.VMEM((2, NZ, 2, SH, W), BF),
            pltpu.VMEM((W, W), BF),
            pltpu.VMEM((W, W), BF),
            pltpu.VMEM((W, W), BF),
            pltpu.VMEM((W, W), BF),
            pltpu.VMEM((W, W), BF),
            pltpu.VMEM((W, W), BF),
            pltpu.VMEM((W, W), BF),
            pltpu.VMEM((W, W), BF),
            pltpu.VMEM((NZ, SH, LANES), F32),
            pltpu.VMEM((4, NZ, 1, LANES), F32),
            pltpu.VMEM((2, CH, W), BF),
            pltpu.VMEM((2, 2, HALF, W), F32),
            pltpu.VMEM((2, 2, CH, W), BF),
            pltpu.VMEM((2, CH, W), F32),
            pltpu.VMEM((2, 2, HALF, W), BF),
            pltpu.VMEM((2, 2, CH, W), BF),
            pltpu.VMEM((2, CH, W), BF),
            pltpu.VMEM((2, CH, W), BF),
            pltpu.VMEM((CH, W), F32),
            pltpu.VMEM((2, 2, NZ, SH, W), F32),
            pltpu.VMEM((2, 2, NZ, SH, W), BF),
            pltpu.VMEM((2, 2, NZ, SH, W), BF),
            pltpu.VMEM((2, 2, NZ, SH, W), BF),
            pltpu.VMEM((2, 2, 4, SH, W), BF),
            pltpu.VMEM((2, 2, 2, SH, W), BF),
            pltpu.VMEM((2, 2, 2, SH, W), BF),
            pltpu.VMEM((2, 2, 2, SH, W), BF),
            pltpu.VMEM((2, 2, SH, W), F32),
            pltpu.VMEM((2, SH, W), BF),
            pltpu.VMEM((2, SH, W), BF),
            pltpu.VMEM((NZ, SH, LANES), F32),
            pltpu.VMEM((NZ, 1, W), F32),
            pltpu.VMEM((4, 1, W), F32),
            pltpu.SemaphoreType.DMA((COPIES,)),
            pltpu.SemaphoreType.DMA((COPIES,)),
            pltpu.SemaphoreType.DMA((4,)),
        ],
        compiler_params=pltpu.CompilerParams(
            collective_id=0, has_side_effects=True, vmem_limit_bytes=58 << 20
        ),
        cost_estimate=pl.CostEstimate(
            flops=12 * W * W * W, bytes_accessed=10 * W * W, transcendentals=CH * W
        ),
    )(tokens, gain, w_in, b_in.reshape(1, 4 * W), w_out.T, cotangent)
    y_branch, input_grad, w_in_grad, w_out_grad, bias_grad, gain_grad = pl.pallas_call(
        hand_over,
        out_shape=results[:5] + (jax.ShapeDtypeStruct((W,), F32),),
        in_specs=[hbm] * 5 + [vmem],
        out_specs=[hbm] * 5 + [vmem],
        scratch_shapes=[pltpu.VMEM(one.shape, one.dtype) for one in results[:5]]
        + [pltpu.SemaphoreType.DMA((10,))],
    )(*outs)
    return (
        y_branch,
        input_grad,
        w_in_grad,
        w_out_grad.T,
        bias_grad.reshape(4 * W),
        gain_grad,
    )


def solution(mesh):
    placed = (
        P(("gy", "gx"), "gz"),
        P("gz"),
        P("gz", ("gx", "gy")),
        P("gx"),
        P("gx", ("gz", "gy")),
        P(("gy", "gx"), "gz"),
    )
    return jax.shard_map(
        shards,
        mesh=mesh,
        in_specs=placed,
        out_specs=(
            P(("gy", "gx"), "gz"),
            P(("gy", "gx"), "gz"),
            P("gz", ("gx", "gy")),
            P("gx", ("gz", "gy")),
            P("gx"),
            P("gz"),
        ),
        check_vma=False,
    )
```

```python
import functools

import jax
import jax.numpy as jnp
from jax import lax
from jax.experimental import pallas as pl
from jax.experimental.pallas import tpu as pltpu
from jax.sharding import PartitionSpec as P

epsilon = 1e-06
MESH = pl.DeviceIdType.MESH
BF = jnp.bfloat16
F32 = jnp.float32
NZ = 8
NX = 4
W = 768
CH = 192
HALF = CH // 2
QUART = HALF // 2
OFFSETS = (0, 1, -1, 2, -2, 3, -3, 4)
PLACE = {d: i for i, d in enumerate(OFFSETS)}
SH = 24
FB = 192
TILE = 256
LANES = 128
PARTS = (slice(0, W // 2), slice(W // 2, W))
COPIES = 210
FEATURES = W * NZ
ROOT = 0.7978845608028654
CUBIC = 0.044715


class Sent:
    def __init__(self, copy):
        self.copy, self.waited = copy, False

    def wait_recv(self):
        if not self.waited:
            self.waited = True
            self.copy.wait_recv()


class Local:
    def __init__(self, copy):
        self.copy, self.waited = copy, False

    def wait(self):
        if not self.waited:
            self.waited = True
            self.copy.wait()


class Net:
    def __init__(self, send_sems, recv_sems, local_sems):
        self.local_sems, self.locals = local_sems, []
        self.send_sems, self.recv_sems = send_sems, recv_sems
        self.count = 0
        self.sent = []

    def send(self, src, dst, **where):
        copy = pltpu.make_async_remote_copy(
            src_ref=src,
            dst_ref=dst,
            send_sem=self.send_sems.at[self.count],
            recv_sem=self.recv_sems.at[self.count],
            device_id=where,
            device_id_type=MESH,
        )
        self.count += 1
        copy.start()
        self.sent.append(Sent(copy))
        return self.sent[-1]

    def local(self, src, dst):
        copy = pltpu.make_async_copy(src, dst, self.local_sems.at[len(self.locals)])
        copy.start()
        self.locals.append(Local(copy))
        return self.locals[-1]

    def drain(self):
        for copy in self.locals:
            copy.wait()
        for sent in self.sent:
            sent.wait_recv()
            sent.copy.wait_send()


def dot(left, right, left_dim, right_dim):
    return lax.dot_general(
        left, right, (((left_dim,), (right_dim,)), ((), ())), preferred_element_type=F32
    )


def rows_of(half, chunk):
    return pl.ds(pl.multiple_of(half * (4 * HALF) + chunk * HALF, HALF), HALF)


def both_halves(ref, chunk):
    return jnp.concatenate([ref[rows_of(half, chunk), :] for half in range(2)], axis=0)


def tiles(body, count=W // TILE, size=TILE):
    def step(i, carry):
        body(pl.ds(pl.multiple_of(i * size, size), size))
        return carry

    lax.fori_loop(0, count, step, 0)


def kernel(
    tok, gain, w_in_hbm, b_in, w_out, cot,
    y_out, in_grad, w_in_grad, w_out_grad, b_grad, g_grad,
    g_cot, g_tok, cot_all, nor_all, act_all, pg_all, w_in, w_full, w_send, w_in_out,
    stat_in, stat_all, far, side_f, side_b, own, relay, inbox, yx_out, yx_in, pre,
    keep, core_out, core_in, z_out, z_in, z_three, z_four, z_two, total, ty_out, ty_in,
    stat2_in, stat2_out, gz_in, gy_in,
    send_sems, recv_sems, local_sems,
):
    z, g, q = lax.axis_index("gx"), lax.axis_index("gy"), lax.axis_index("gz")
    yl, c = lax.div(g, 2), lax.rem(g, 2)
    x, h = lax.div(q, 2), lax.rem(q, 2)
    net = Net(send_sems, recv_sems, local_sems)

    def ring(value, step, size):
        return lax.rem(value + (step + size), size)

    def z_at(step):
        return ring(z, step, NZ)

    def q_at(step):
        return ring(q, step, NZ)

    def g_at(step):
        return ring(g, step, 4)

    def x_at(step):
        return ring(x, step, NX)

    def x_dev(step):
        return x_at(step) * 2 + h

    y_peer = (1 - yl) * 2 + c
    core_peer = yl * 2 + (1 - c)
    h_peer = x * 2 + (1 - h)

    def hidden_of(group):
        return pl.ds(pl.multiple_of(group * W, W), W)

    def features_of(group):
        return pl.ds(pl.multiple_of(group * FB, FB), FB)

    load_w_in = net.local(w_in_hbm, w_in)
    load_w_out = net.local(w_out.at[:, hidden_of(g)], w_full.at[features_of(g)])

    barrier = pltpu.get_barrier_semaphore()
    for s in range(1, NZ):
        pl.semaphore_signal(barrier, inc=1, device_id={"gx": z_at(s)}, device_id_type=MESH)
        pl.semaphore_signal(barrier, inc=1, device_id={"gz": q_at(s)}, device_id_type=MESH)
        where = {"gy": y_peer, "gz": q_at(s)}
        pl.semaphore_signal(barrier, inc=1, device_id=where, device_id_type=MESH)
    for s in range(1, 4):
        pl.semaphore_signal(barrier, inc=1, device_id={"gy": g_at(s)}, device_id_type=MESH)

    lane = lax.broadcasted_iota(jnp.int32, (SH, LANES), 1)
    row = lax.broadcasted_iota(jnp.int32, (SH, LANES), 0)
    MID = LANES // 2

    def pair_tile(first, second):
        return jnp.where(lane < MID, first, second)

    def split_pair(both):
        return both[:, 0:1], both[:, MID : MID + 1]

    floats = tok[...].astype(F32)
    stat_in[0] = pair_tile(
        jnp.sum(floats, 1, keepdims=True), jnp.sum(floats * floats, 1, keepdims=True)
    )
    g_tok[c, z, yl] = tok[...]
    g_cot[c, z, yl] = cot[...]
    pl.semaphore_wait(barrier, 3 * (NZ - 1) + 3)

    stats = [net.send(stat_in.at[0], stat_in.at[s], gz=q_at(s)) for s in range(1, NZ)]

    class Lane:
        def __init__(self, which):
            self.which, self.right, self.left = which, {}, {}
            self.forward(0, True, True)

        def forward(self, step, right, left):
            block = g_tok.at[c, z_at(step), self.which]
            if right:
                self.right[1 - step] = net.send(block, block, gx=z_at(1))
            if left:
                self.left[1 + step] = net.send(block, block, gx=z_at(-1))

        def onward(self, n):
            self.right[n].wait_recv()
            self.forward(-n, n < 4, False)
            if n < 4:
                self.left[n].wait_recv()
                self.forward(n, False, n < 3)

    def normalise(half):
        offsets = OFFSETS[4 * half : 4 * half + 4]
        for d in offsets:
            tok_cores[-4 if d == 4 else d].wait_recv()
        for group in range(4):
            rows = [
                centred_rows(group // 2, group % 2, z_at(d)) * gain_row() for d in offsets
            ]
            nor_all[rows_of(half, group), :] = jnp.concatenate(rows, 0).astype(BF)

    def tok_to_core(step):
        block = g_tok.at[c, z_at(step)]
        tok_cores[step] = net.send(block, block, gy=core_peer)

    class Gather:
        def __init__(self, buf):
            self.buf = buf
            self.first = net.send(buf.at[c, z, yl], buf.at[c, z, yl], gy=y_peer)
            self.right, self.left, self.cores = {}, {}, []

        def forward(self, step, right, left):
            block = self.buf.at[c, z_at(step)]
            if right:
                self.right[1 - step] = net.send(block, block, gx=z_at(1))
            if left:
                self.left[1 + step] = net.send(block, block, gx=z_at(-1))
            self.cores.append(net.send(block, block, gy=core_peer))

        def begin(self):
            self.first.wait_recv()
            self.forward(0, True, True)

        def onward(self, n):
            self.right[n].wait_recv()
            self.forward(-n, n < 4, False)
            if n < 4:
                self.left[n].wait_recv()
                self.forward(n, False, n < 3)

        def finish(self, whole):
            for copy in self.cores:
                copy.wait_recv()
            for half in range(2):
                for group in range(4):
                    piece = self.buf.at[group % 2, :, group // 2]
                    rows = [
                        piece[z_at(d)].astype(F32) for d in OFFSETS[4 * half : 4 * half + 4]
                    ]
                    whole[rows_of(half, group), :] = jnp.concatenate(rows, 0).astype(BF)

    tok_cores = {}
    tok_y = net.send(g_tok.at[c, z, yl], g_tok.at[c, z, yl], gy=y_peer)
    near = Lane(yl)
    cots = Gather(g_cot)

    def turn(half):
        part = pl.ds(half * (FB // 2), FB // 2)
        rows = pl.ds(pl.multiple_of(g * FB + half * (FB // 2), FB // 2), FB // 2)
        return [
            net.send(w_out.at[part, hidden_of(g_at(s))], w_full.at[rows], gy=g_at(s))
            for s in range(1, 4)
        ]

    turned = turn(0)
    tok_y.wait_recv()
    across = Lane(1 - yl)
    tok_to_core(0)
    near.onward(1)
    cots.begin()
    for copy in stats:
        copy.wait_recv()
    both = stat_in[0]
    for s in range(1, NZ):
        both = both + stat_in[s]
    row_sum, row_square = split_pair(both)
    row_mean = row_sum / FEATURES
    row_var = row_square / FEATURES - row_mean * row_mean
    inv_std = lax.rsqrt(row_var + epsilon)

    def gain_row():
        return gain[...].reshape(1, W)

    def centre():
        return (tok[...].astype(F32) - row_mean) * inv_std

    on_row = lane == row
    on_mid = lane == row + MID

    def centred_rows(low, core, where):
        means, scales = unpack(stat_all[2 * low + core, where])
        return (g_tok[core, where, low].astype(F32) - means) * scales

    def pack(first, second):
        both = jnp.where(on_row, first, 0.0) + jnp.where(on_mid, second, 0.0)
        return jnp.sum(both, 0, keepdims=True)

    def unpack(packed):
        first = jnp.sum(jnp.where(on_row, packed, 0.0), 1, keepdims=True)
        return first, jnp.sum(jnp.where(on_mid, packed, 0.0), 1, keepdims=True)

    stat_all[g, z] = pack(row_mean, inv_std)
    stats = [net.send(stat_all.at[g, z], stat_all.at[g, z], gx=z_at(s)) for s in range(1, NZ)]

    across.onward(1)
    tok_to_core(1)
    tok_to_core(-1)
    near.onward(2)
    for copy in stats:
        copy.wait_recv()
    stats = [net.send(stat_all.at[g], stat_all.at[g], gy=g_at(s)) for s in range(1, 4)]
    turned += turn(1)
    across.onward(2)
    tok_to_core(2)
    tok_to_core(-2)
    cots.onward(1)
    near.onward(3)
    for copy in stats:
        copy.wait_recv()
    class HiddenSum:
        def __init__(self, n, half, product):
            self.n, self.half, self.product = 2 * n + half, half, product

        def begin(self, between=()):
            n, half = self.n, self.half

            def far_tile(cols):
                far[n, :, cols] = self.product(half, x_at(2), cols).astype(BF)

            tiles(far_tile)
            self.relays = [
                net.send(
                    far.at[n, pl.ds(side * QUART, QUART)], relay.at[n, side], gz=x_dev(step)
                )
                for side, step in enumerate((1, -1))
            ]
            for action in between:
                action()
            self.raw = []
            for side, step in enumerate((1, -1)):

                def side_tile(cols):
                    value = self.product(half, x_at(step), cols)
                    side_f[n, side, :, cols] = value[side * QUART : (side + 1) * QUART]
                    other = 1 - side
                    side_b[n, side, pl.ds(other * QUART, QUART), cols] = value[
                        other * QUART : (other + 1) * QUART
                    ].astype(BF)

                tiles(side_tile)
                part = pl.ds((1 - side) * QUART, QUART)
                self.raw.append(
                    net.send(side_b.at[n, side, part], inbox.at[n, side, part], gz=x_dev(step))
                )

            def own_tile(cols):
                own[n, :, cols] = self.product(half, x, cols)

            tiles(own_tile)

        def relayed(self):
            n = self.n
            self.summed = []
            for side, step in enumerate((1, -1)):
                self.relays[side].wait_recv()
                part = pl.ds(side * QUART, QUART)

                def add_tile(cols):
                    value = side_f[n, side, :, cols] + relay[n, side, :, cols].astype(F32)
                    side_b[n, side, part, cols] = value.astype(BF)

                tiles(add_tile)
                self.summed.append(
                    net.send(side_b.at[n, side, part], inbox.at[n, side, part], gz=x_dev(step))
                )

        def pair_up(self):
            n = self.n
            for copy in self.raw + self.summed:
                copy.wait_recv()

            def add_tile(cols):
                value = own[n, :, cols] + inbox[n, 0, :, cols].astype(F32)
                yx_out[n, :, cols] = (value + inbox[n, 1, :, cols].astype(F32)).astype(BF)

            tiles(add_tile)
            self.pair = net.send(yx_out.at[n], yx_in.at[n], gz=h_peer)

        def total(self, rows):
            n = self.n
            return yx_out[n, rows, :].astype(F32) + yx_in[n, rows, :].astype(F32)

    def pre_product(half, k, cols):
        return dot(nor_all[rows_of(half, k), :], w_in[:, cols], 1, 0)

    def grad_product(half, k, cols):
        return dot(cot_all[rows_of(half, k), :], w_full[:, cols], 1, 0)

    pres = [HiddenSum(0, half, pre_product) for half in range(2)]
    grads = [HiddenSum(1, half, grad_product) for half in range(2)]

    def across_three():
        across.onward(3)
        tok_to_core(3)
        tok_to_core(-3)

    def cots_two():
        cots.onward(2)

    normalise(0)
    load_w_in.wait()
    pres[0].begin([across_three, cots_two])
    near.onward(4)
    across.onward(4)
    tok_to_core(-4)
    normalise(1)
    pres[0].relayed()
    pres[1].begin([lambda: cots.onward(3)])
    pres[0].pair_up()
    cots.onward(4)
    pres[1].relayed()
    cots.finish(cot_all)
    for copy in turned:
        copy.wait_recv()
    load_w_out.wait()
    grads[0].begin()

    bias = b_in[:, pl.ds(pl.multiple_of(g * W, W), W)]

    class HiddenGather:
        def __init__(self, whole):
            self.whole, self.sides, self.onwards = whole, {}, []

        def begin(self, half):
            rows = self.whole.at[rows_of(half, x)]
            for side, step in enumerate((1, -1)):
                self.sides[side, half] = net.send(rows, rows, gz=x_dev(step))

        def onward(self):
            for side, step in enumerate((1, -1)):
                self.sides[side, side].wait_recv()
                rows = self.whole.at[rows_of(side, x_at(-step))]
                self.onwards.append(net.send(rows, rows, gz=x_dev(step)))

        def neighbours(self):
            for copy in self.sides.values():
                copy.wait_recv()

        def finish(self):
            for copy in self.onwards:
                copy.wait_recv()

    acts, pgs = HiddenGather(act_all), HiddenGather(pg_all)

    class FeatureSum:
        def __init__(self, n, product):
            self.n, self.product = n, product
            self.cores, self.three, self.four, self.last_hops = {}, {}, {}, {}

        def target(self, order):
            return lax.div(x, 2) if order == 0 else 1 - lax.div(x, 2)

        def products(self, order):
            n, j = self.n, self.target(order)

            def send_tile(cols):
                value = self.product(2 * j + (1 - c), cols)
                core_out[n, order, :, :, cols] = value.reshape(NZ, SH, TILE).astype(BF)

            tiles(send_tile)
            self.cores[order] = net.send(
                core_out.at[n, order], core_in.at[n, order], gy=core_peer
            )

            def keep_tile(cols):
                value = self.product(2 * j + c, cols)
                keep[n, order, :, :, cols] = value.reshape(NZ, SH, TILE)

            tiles(keep_tile)

        def scatter(self, order):
            n = self.n
            self.cores[order].wait_recv()

            def add_one(i, carry):
                value = keep[n, order, i] + core_in[n, order, i].astype(F32)
                keep[n, order, i] = value
                z_out[n, order, i] = value.astype(BF)
                return carry

            lax.fori_loop(0, NZ, add_one, 0)
            out, sides = z_out.at[n, order], tuple(enumerate((1, -1)))
            self.three[order] = [
                net.send(out.at[PLACE[3 * d]], z_three.at[n, order, i], gx=z_at(d))
                for i, d in sides
            ]
            self.four[order] = [
                net.send(
                    out.at[PLACE[4], :, part], z_four.at[n, order, i, :, part], gx=z_at(2 * d)
                )
                for (i, d), part in zip(sides, PARTS)
            ]
            self.last_hops[order] = [
                net.send(out.at[PLACE[d]], z_in.at[n, order, i], gx=z_at(d)) for i, d in sides
            ]

        def relay(self, order):
            n = self.n
            for i, d in enumerate((1, -1)):
                self.three[order][i].wait_recv()
                self.four[order][i].wait_recv()
                for k, part in enumerate(PARTS):
                    value = keep[n, order, PLACE[2 * d], :, part]
                    value = value + z_three[n, order, i, :, part].astype(F32)
                    if k == i:
                        value = value + z_four[n, order, i, :, part].astype(F32)
                    z_two[n, order, i, :, part] = value.astype(BF)
                self.last_hops[order].append(
                    net.send(z_two.at[n, order, i], z_in.at[n, order, 2 + i], gx=z_at(2 * d))
                )

        def collect(self, order):
            n = self.n
            for copy in self.last_hops[order]:
                copy.wait_recv()
            value = keep[n, order, 0]
            for s in range(4):
                value = value + z_in[n, order, s].astype(F32)
            total[n, order] = value

        def exchange(self):
            n = self.n
            here = lax.rem(lax.div(x, 2) + yl, 2)
            ty_out[n] = total[n, 1 - here].astype(BF)
            self.last = net.send(ty_out.at[n], ty_in.at[n], gy=y_peer)
            self.here = here

        def result(self):
            self.last.wait_recv()
            return total[self.n, self.here] + ty_in[self.n].astype(F32)

    ys = FeatureSum(0, lambda k, cols: dot(both_halves(act_all, k), w_full[cols, :], 1, 1))
    norms = FeatureSum(1, lambda k, cols: dot(both_halves(pg_all, k), w_in[cols, :], 1, 1))

    STEP = 32

    def activate(half):
        pres[half].pair.wait_recv()

        def one(i, carry):
            start = pl.multiple_of(i * STEP, STEP)
            rows = pl.ds(start, STEP)
            v = pres[half].total(rows) + bias
            t = jnp.tanh(ROOT * (v + CUBIC * v * v * v))
            place = pl.multiple_of(half * (4 * HALF) + x * HALF + start, STEP)
            act_all[pl.ds(place, STEP), :] = (0.5 * v * (1.0 + t)).astype(BF)
            pre[half, rows, :] = 0.5 * (1.0 + t) + 0.5 * v * (1.0 - t * t) * ROOT * (
                1.0 + 3.0 * CUBIC * v * v
            )
            return carry

        lax.fori_loop(0, HALF // STEP, one, 0)
        acts.begin(half)

    def backward(half):
        grads[half].pair.wait_recv()

        def one(i, carry):
            start = pl.multiple_of(i * STEP, STEP)
            rows = pl.ds(start, STEP)
            place = pl.multiple_of(half * (4 * HALF) + x * HALF + start, STEP)
            pg_all[pl.ds(place, STEP), :] = (
                grads[half].total(rows) * pre[half, rows, :]
            ).astype(BF)
            return carry

        lax.fori_loop(0, HALF // STEP, one, 0)
        pgs.begin(half)

    pres[1].pair_up()
    activate(0)
    grads[0].relayed()
    grads[1].begin()
    grads[0].pair_up()
    activate(1)
    grads[1].relayed()
    backward(0)
    grads[1].pair_up()
    acts.onward()
    acts.neighbours()
    ys.products(0)
    backward(1)
    ys.scatter(0)
    acts.finish()
    ys.products(1)

    def w_out_tile(rows):
        w_send[rows, :] = dot(cot_all[:, rows], act_all[...], 0, 0).astype(BF)

    tiles(w_out_tile)
    for s in range(1, 4):
        net.send(
            w_send.at[features_of(g_at(s))], w_out_grad.at[:, hidden_of(g)], gy=g_at(s)
        )
    net.local(w_send.at[features_of(g)], w_out_grad.at[:, hidden_of(g)])
    pgs.onward()
    ys.relay(0)
    ys.scatter(1)
    pgs.neighbours()
    norms.products(0)
    ys.relay(1)
    norms.scatter(0)
    ys.collect(0)
    ys.collect(1)
    ys.exchange()
    pgs.finish()
    norms.products(1)
    norms.relay(0)
    norms.scatter(1)

    def bias_sum(i, carry):
        rows = pl.ds(pl.multiple_of(i * STEP, STEP), STEP)
        return carry + jnp.sum(pg_all[rows, :].astype(F32), 0, keepdims=True)

    b_grad[g] = lax.fori_loop(0, W // STEP, bias_sum, jnp.zeros((1, W), F32))
    biases = [net.send(b_grad.at[g], b_grad.at[g], gy=g_at(s)) for s in range(1, 4)]

    def w_in_tile(rows):
        w_in_out[rows, :] = dot(nor_all[:, rows], pg_all[...], 0, 0).astype(BF)

    tiles(w_in_tile)
    net.local(w_in_out, w_in_grad)

    norms.relay(1)
    norms.collect(0)
    norms.collect(1)
    norms.exchange()
    partial = jnp.zeros((1, W), F32)
    for order in range(2):
        value = total[1, order]
        centred = centred_rows(norms.target(order), c, z)
        partial = partial + jnp.sum(value * centred, 0, keepdims=True)
        value = value * gain_row()
        stat2_out[order] = pack(
            jnp.sum(value, 1, keepdims=True), jnp.sum(value * centred, 1, keepdims=True)
        )
    mine, other = norms.here, 1 - norms.here
    stats2 = [
        net.send(stat2_out.at[mine], stat2_in.at[s], gz=q_at(s)) for s in range(1, NZ)
    ] + [
        net.send(stat2_out.at[other], stat2_in.at[NZ + s], gy=y_peer, gz=q_at(s))
        for s in range(NZ)
    ]
    stat2_in[0] = stat2_out[mine]
    gz_in[z] = partial
    gains = [net.send(gz_in.at[z], gz_in.at[z], gx=z_at(s)) for s in range(1, NZ)]
    y_out[...] = ys.result().astype(BF)

    norm_grad = norms.result()
    centred = centre()
    hat_grad = norm_grad * gain_row()
    for copy in gains:
        copy.wait_recv()
    value = gz_in[0]
    for i in range(1, NZ):
        value = value + gz_in[i]
    gy_in[g] = value
    gains = [net.send(gy_in.at[g], gy_in.at[g], gy=g_at(s)) for s in range(1, 4)]
    for copy in stats2:
        copy.wait_recv()
    packed = stat2_in[0]
    for s in range(1, 2 * NZ):
        packed = packed + stat2_in[s]
    first, second = unpack(packed)
    in_grad[...] = (
        (hat_grad - first / FEATURES - centred * (second / FEATURES)) * inv_std
    ).astype(BF)
    for copy in gains:
        copy.wait_recv()
    g_grad[...] = (gy_in[0] + gy_in[1]) + (gy_in[2] + gy_in[3])
    net.drain()


def hand_over(*refs):
    ins, outs, held, sems = refs[:6], refs[6:12], refs[12:17], refs[17]
    order = (2, 3, 0, 1, 4)
    first = {i: pltpu.make_async_copy(ins[i], held[i], sems.at[i]) for i in order}
    second = {i: pltpu.make_async_copy(held[i], outs[i], sems.at[5 + i]) for i in order}
    for i in order:
        first[i].start()
    outs[5][...] = ins[5][...].reshape(W)
    for i in order:
        first[i].wait()
        second[i].start()
    for i in order:
        second[i].wait()


def shards(tokens, gain, w_in, b_in, w_out, cotangent):
    vmem = pl.BlockSpec(memory_space=pltpu.VMEM)
    hbm = pl.BlockSpec(memory_space=pl.ANY)
    results = (
        jax.ShapeDtypeStruct((SH, W), BF),
        jax.ShapeDtypeStruct((SH, W), BF),
        jax.ShapeDtypeStruct((W, W), BF),
        jax.ShapeDtypeStruct((FB, 4 * W), BF),
        jax.ShapeDtypeStruct((4, 1, W), F32),
        jax.ShapeDtypeStruct((1, W), F32),
    )
    outs = pl.pallas_call(
        kernel,
        out_shape=results,
        in_specs=[vmem, vmem, hbm, vmem, hbm, vmem],
        out_specs=[vmem, vmem, hbm, hbm, vmem, vmem],
        scratch_shapes=[
            pltpu.VMEM((2, NZ, 2, SH, W), BF),
            pltpu.VMEM((2, NZ, 2, SH, W), BF),
            pltpu.VMEM((W, W), BF),
            pltpu.VMEM((W, W), BF),
            pltpu.VMEM((W, W), BF),
            pltpu.VMEM((W, W), BF),
            pltpu.VMEM((W, W), BF),
            pltpu.VMEM((W, W), BF),
            pltpu.VMEM((W, W), BF),
            pltpu.VMEM((W, W), BF),
            pltpu.VMEM((NZ, SH, LANES), F32),
            pltpu.VMEM((4, NZ, 1, LANES), F32),
            pltpu.VMEM((4, HALF, W), BF),
            pltpu.VMEM((4, 2, QUART, W), F32),
            pltpu.VMEM((4, 2, HALF, W), BF),
            pltpu.VMEM((4, HALF, W), F32),
            pltpu.VMEM((4, 2, QUART, W), BF),
            pltpu.VMEM((4, 2, HALF, W), BF),
            pltpu.VMEM((4, HALF, W), BF),
            pltpu.VMEM((4, HALF, W), BF),
            pltpu.VMEM((2, HALF, W), F32),
            pltpu.VMEM((2, 2, NZ, SH, W), F32),
            pltpu.VMEM((2, 2, NZ, SH, W), BF),
            pltpu.VMEM((2, 2, NZ, SH, W), BF),
            pltpu.VMEM((2, 2, NZ, SH, W), BF),
            pltpu.VMEM((2, 2, 4, SH, W), BF),
            pltpu.VMEM((2, 2, 2, SH, W), BF),
            pltpu.VMEM((2, 2, 2, SH, W), BF),
            pltpu.VMEM((2, 2, 2, SH, W), BF),
            pltpu.VMEM((2, 2, SH, W), F32),
            pltpu.VMEM((2, SH, W), BF),
            pltpu.VMEM((2, SH, W), BF),
            pltpu.VMEM((2 * NZ, 1, LANES), F32),
            pltpu.VMEM((2, 1, LANES), F32),
            pltpu.VMEM((NZ, 1, W), F32),
            pltpu.VMEM((4, 1, W), F32),
            pltpu.SemaphoreType.DMA((COPIES,)),
            pltpu.SemaphoreType.DMA((COPIES,)),
            pltpu.SemaphoreType.DMA((4,)),
        ],
        compiler_params=pltpu.CompilerParams(
            collective_id=0, has_side_effects=True, vmem_limit_bytes=58 << 20
        ),
        cost_estimate=pl.CostEstimate(
            flops=12 * W * W * W, bytes_accessed=10 * W * W, transcendentals=CH * W
        ),
    )(tokens, gain, w_in, b_in.reshape(1, 4 * W), w_out.T, cotangent)
    y_branch, input_grad, w_in_grad, w_out_grad, bias_grad, gain_grad = pl.pallas_call(
        hand_over,
        out_shape=results[:5] + (jax.ShapeDtypeStruct((W,), F32),),
        in_specs=[hbm] * 5 + [vmem],
        out_specs=[hbm] * 5 + [vmem],
        scratch_shapes=[pltpu.VMEM(one.shape, one.dtype) for one in results[:5]]
        + [pltpu.SemaphoreType.DMA((10,))],
    )(*outs)
    return (
        y_branch,
        input_grad,
        w_in_grad,
        w_out_grad.T,
        bias_grad.reshape(4 * W),
        gain_grad,
    )


def solution(mesh):
    placed = (
        P(("gy", "gx"), "gz"),
        P("gz"),
        P("gz", ("gx", "gy")),
        P("gx"),
        P("gx", ("gz", "gy")),
        P(("gy", "gx"), "gz"),
    )
    return jax.shard_map(
        shards,
        mesh=mesh,
        in_specs=placed,
        out_specs=(
            P(("gy", "gx"), "gz"),
            P(("gy", "gx"), "gz"),
            P("gz", ("gx", "gy")),
            P("gx", ("gz", "gy")),
            P("gx"),
            P("gz"),
        ),
        check_vma=False,
    )
```

```python
import functools

import jax
import jax.numpy as jnp
from jax import lax
from jax.experimental import pallas as pl
from jax.experimental.pallas import tpu as pltpu
from jax.sharding import PartitionSpec as P

epsilon = 1e-06
MESH = pl.DeviceIdType.MESH
BF = jnp.bfloat16
F32 = jnp.float32
NZ = 8
NX = 4
W = 768
CH = 192
HALF = CH // 2
QUART = HALF // 2
OFFSETS = (0, 1, -1, 2, -2, 3, -3, 4)
PLACE = {d: i for i, d in enumerate(OFFSETS)}
SH = 24
FB = 192
TILE = 256
LANES = 128
PARTS = (slice(0, W // 2), slice(W // 2, W))
COPIES = 210
FEATURES = W * NZ
ROOT = 0.7978845608028654
CUBIC = 0.044715


class Sent:
    def __init__(self, copy):
        self.copy, self.waited = copy, False

    def wait_recv(self):
        if not self.waited:
            self.waited = True
            self.copy.wait_recv()


class Local:
    def __init__(self, copy):
        self.copy, self.waited = copy, False

    def wait(self):
        if not self.waited:
            self.waited = True
            self.copy.wait()


class Net:
    def __init__(self, send_sems, recv_sems, local_sems):
        self.local_sems, self.locals = local_sems, []
        self.send_sems, self.recv_sems = send_sems, recv_sems
        self.count = 0
        self.sent = []

    def send(self, src, dst, **where):
        copy = pltpu.make_async_remote_copy(
            src_ref=src,
            dst_ref=dst,
            send_sem=self.send_sems.at[self.count],
            recv_sem=self.recv_sems.at[self.count],
            device_id=where,
            device_id_type=MESH,
        )
        self.count += 1
        copy.start()
        self.sent.append(Sent(copy))
        return self.sent[-1]

    def local(self, src, dst):
        copy = pltpu.make_async_copy(src, dst, self.local_sems.at[len(self.locals)])
        copy.start()
        self.locals.append(Local(copy))
        return self.locals[-1]

    def drain(self):
        for copy in self.locals:
            copy.wait()
        for sent in self.sent:
            sent.wait_recv()
            sent.copy.wait_send()


def dot(left, right, left_dim, right_dim):
    return lax.dot_general(
        left, right, (((left_dim,), (right_dim,)), ((), ())), preferred_element_type=F32
    )


def rows_of(half, chunk):
    return pl.ds(pl.multiple_of(half * (4 * HALF) + chunk * HALF, HALF), HALF)


def both_halves(ref, chunk):
    return jnp.concatenate([ref[rows_of(half, chunk), :] for half in range(2)], axis=0)


def tiles(body, count=W // TILE, size=TILE):
    def step(i, carry):
        body(pl.ds(pl.multiple_of(i * size, size), size))
        return carry

    lax.fori_loop(0, count, step, 0)


def kernel(
    tok, gain, w_in_hbm, b_in, w_out, cot,
    y_out, in_grad, w_in_grad, w_out_grad, b_grad, g_grad,
    g_cot, g_tok, cot_all, nor_all, act_all, pg_all, w_in, w_full, w_send, w_in_out,
    stat_in, stat_all, far, side_f, side_b, own, relay, inbox, yx_out, yx_in, pre,
    keep, core_out, core_in, z_out, z_in, z_three, z_four, z_two, total, ty_out, ty_in,
    stat2_in, stat2_out, gz_in, gy_in,
    send_sems, recv_sems, local_sems,
):
    z, g, q = lax.axis_index("gx"), lax.axis_index("gy"), lax.axis_index("gz")
    yl, c = lax.div(g, 2), lax.rem(g, 2)
    x, h = lax.div(q, 2), lax.rem(q, 2)
    net = Net(send_sems, recv_sems, local_sems)

    def ring(value, step, size):
        return lax.rem(value + (step + size), size)

    def z_at(step):
        return ring(z, step, NZ)

    def q_at(step):
        return ring(q, step, NZ)

    def g_at(step):
        return ring(g, step, 4)

    def x_at(step):
        return ring(x, step, NX)

    def x_dev(step):
        return x_at(step) * 2 + h

    y_peer = (1 - yl) * 2 + c
    core_peer = yl * 2 + (1 - c)
    h_peer = x * 2 + (1 - h)

    def hidden_of(group):
        return pl.ds(pl.multiple_of(group * W, W), W)

    def features_of(group):
        return pl.ds(pl.multiple_of(group * FB, FB), FB)

    load_w_in = net.local(w_in_hbm, w_in)
    load_w_out = net.local(w_out.at[:, hidden_of(g)], w_full.at[features_of(g)])

    barrier = pltpu.get_barrier_semaphore()
    for s in range(1, NZ):
        pl.semaphore_signal(barrier, inc=1, device_id={"gx": z_at(s)}, device_id_type=MESH)
        pl.semaphore_signal(barrier, inc=1, device_id={"gz": q_at(s)}, device_id_type=MESH)
        where = {"gy": y_peer, "gz": q_at(s)}
        pl.semaphore_signal(barrier, inc=1, device_id=where, device_id_type=MESH)
    for s in range(1, 4):
        pl.semaphore_signal(barrier, inc=1, device_id={"gy": g_at(s)}, device_id_type=MESH)

    lane = lax.broadcasted_iota(jnp.int32, (SH, LANES), 1)
    row = lax.broadcasted_iota(jnp.int32, (SH, LANES), 0)
    MID = LANES // 2

    def pair_tile(first, second):
        return jnp.where(lane < MID, first, second)

    def split_pair(both):
        return both[:, 0:1], both[:, MID : MID + 1]

    floats = tok[...].astype(F32)
    stat_in[0] = pair_tile(
        jnp.sum(floats, 1, keepdims=True), jnp.sum(floats * floats, 1, keepdims=True)
    )
    g_tok[c, z, yl] = tok[...]
    g_cot[c, z, yl] = cot[...]
    pl.semaphore_wait(barrier, 3 * (NZ - 1) + 3)

    stats = [net.send(stat_in.at[0], stat_in.at[s], gz=q_at(s)) for s in range(1, NZ)]

    class Lane:
        def __init__(self, which):
            self.which, self.right, self.left = which, {}, {}
            self.forward(0, True, True)

        def forward(self, step, right, left):
            block = g_tok.at[c, z_at(step), self.which]
            if right:
                self.right[1 - step] = net.send(block, block, gx=z_at(1))
            if left:
                self.left[1 + step] = net.send(block, block, gx=z_at(-1))

        def onward(self, n):
            self.right[n].wait_recv()
            self.forward(-n, n < 4, False)
            if n < 4:
                self.left[n].wait_recv()
                self.forward(n, False, n < 3)

    def normalise(half):
        offsets = OFFSETS[4 * half : 4 * half + 4]
        for d in offsets:
            tok_cores[-4 if d == 4 else d].wait_recv()
        for group in range(4):
            rows = [
                centred_rows(group // 2, group % 2, z_at(d)) * gain_row() for d in offsets
            ]
            nor_all[rows_of(half, group), :] = jnp.concatenate(rows, 0).astype(BF)

    def tok_to_core(step):
        block = g_tok.at[c, z_at(step)]
        tok_cores[step] = net.send(block, block, gy=core_peer)

    class Gather:
        def __init__(self, buf):
            self.buf = buf
            self.first = net.send(buf.at[c, z, yl], buf.at[c, z, yl], gy=y_peer)
            self.right, self.left, self.cores = {}, {}, []

        def forward(self, step, right, left):
            block = self.buf.at[c, z_at(step)]
            if right:
                self.right[1 - step] = net.send(block, block, gx=z_at(1))
            if left:
                self.left[1 + step] = net.send(block, block, gx=z_at(-1))
            self.cores.append(net.send(block, block, gy=core_peer))

        def begin(self):
            self.first.wait_recv()
            self.forward(0, True, True)

        def onward(self, n):
            self.right[n].wait_recv()
            self.forward(-n, n < 4, False)
            if n < 4:
                self.left[n].wait_recv()
                self.forward(n, False, n < 3)

        def finish(self, whole):
            for copy in self.cores:
                copy.wait_recv()
            for half in range(2):
                for group in range(4):
                    piece = self.buf.at[group % 2, :, group // 2]
                    rows = [
                        piece[z_at(d)].astype(F32) for d in OFFSETS[4 * half : 4 * half + 4]
                    ]
                    whole[rows_of(half, group), :] = jnp.concatenate(rows, 0).astype(BF)

    tok_cores = {}
    tok_y = net.send(g_tok.at[c, z, yl], g_tok.at[c, z, yl], gy=y_peer)
    near = Lane(yl)
    cots = Gather(g_cot)

    def turn(half):
        part = pl.ds(half * (FB // 2), FB // 2)
        rows = pl.ds(pl.multiple_of(g * FB + half * (FB // 2), FB // 2), FB // 2)
        return [
            net.send(w_out.at[part, hidden_of(g_at(s))], w_full.at[rows], gy=g_at(s))
            for s in range(1, 4)
        ]

    turned = turn(0)
    tok_y.wait_recv()
    across = Lane(1 - yl)
    tok_to_core(0)
    near.onward(1)
    cots.begin()
    for copy in stats:
        copy.wait_recv()
    both = stat_in[0]
    for s in range(1, NZ):
        both = both + stat_in[s]
    row_sum, row_square = split_pair(both)
    row_mean = row_sum / FEATURES
    row_var = row_square / FEATURES - row_mean * row_mean
    inv_std = lax.rsqrt(row_var + epsilon)

    def gain_row():
        return gain[...].reshape(1, W)

    def centre():
        return (tok[...].astype(F32) - row_mean) * inv_std

    on_row = lane == row
    on_mid = lane == row + MID

    def centred_rows(low, core, where):
        means, scales = unpack(stat_all[2 * low + core, where])
        return (g_tok[core, where, low].astype(F32) - means) * scales

    def pack(first, second):
        both = jnp.where(on_row, first, 0.0) + jnp.where(on_mid, second, 0.0)
        return jnp.sum(both, 0, keepdims=True)

    def unpack(packed):
        first = jnp.sum(jnp.where(on_row, packed, 0.0), 1, keepdims=True)
        return first, jnp.sum(jnp.where(on_mid, packed, 0.0), 1, keepdims=True)

    stat_all[g, z] = pack(row_mean, inv_std)
    stats = [net.send(stat_all.at[g, z], stat_all.at[g, z], gx=z_at(s)) for s in range(1, NZ)]

    across.onward(1)
    tok_to_core(1)
    tok_to_core(-1)
    near.onward(2)
    for copy in stats:
        copy.wait_recv()
    stats = [net.send(stat_all.at[g], stat_all.at[g], gy=g_at(s)) for s in range(1, 4)]
    turned += turn(1)
    across.onward(2)
    tok_to_core(2)
    tok_to_core(-2)
    cots.onward(1)
    near.onward(3)
    for copy in stats:
        copy.wait_recv()
    class HiddenSum:
        def __init__(self, n, half, product):
            self.n, self.half, self.product = 2 * n + half, half, product

        def begin(self, between=()):
            n, half = self.n, self.half

            def far_tile(cols):
                far[n, :, cols] = self.product(half, x_at(2), cols).astype(BF)

            tiles(far_tile)
            self.relays = [
                net.send(
                    far.at[n, pl.ds(side * QUART, QUART)], relay.at[n, side], gz=x_dev(step)
                )
                for side, step in enumerate((1, -1))
            ]
            for action in between:
                action()
            self.raw = []
            for side, step in enumerate((1, -1)):

                def side_tile(cols):
                    value = self.product(half, x_at(step), cols)
                    side_f[n, side, :, cols] = value[side * QUART : (side + 1) * QUART]
                    other = 1 - side
                    side_b[n, side, pl.ds(other * QUART, QUART), cols] = value[
                        other * QUART : (other + 1) * QUART
                    ].astype(BF)

                tiles(side_tile)
                part = pl.ds((1 - side) * QUART, QUART)
                self.raw.append(
                    net.send(side_b.at[n, side, part], inbox.at[n, side, part], gz=x_dev(step))
                )

            def own_tile(cols):
                own[n, :, cols] = self.product(half, x, cols)

            tiles(own_tile)

        def relayed(self):
            n = self.n
            self.summed = []
            for side, step in enumerate((1, -1)):
                self.relays[side].wait_recv()
                part = pl.ds(side * QUART, QUART)

                def add_tile(cols):
                    value = side_f[n, side, :, cols] + relay[n, side, :, cols].astype(F32)
                    side_b[n, side, part, cols] = value.astype(BF)

                tiles(add_tile)
                self.summed.append(
                    net.send(side_b.at[n, side, part], inbox.at[n, side, part], gz=x_dev(step))
                )

        def pair_up(self):
            n = self.n
            for copy in self.raw + self.summed:
                copy.wait_recv()

            def add_tile(cols):
                value = own[n, :, cols] + inbox[n, 0, :, cols].astype(F32)
                yx_out[n, :, cols] = (value + inbox[n, 1, :, cols].astype(F32)).astype(BF)

            tiles(add_tile)
            self.pair = net.send(yx_out.at[n], yx_in.at[n], gz=h_peer)

        def total(self, rows):
            n = self.n
            return yx_out[n, rows, :].astype(F32) + yx_in[n, rows, :].astype(F32)

    def pre_product(half, k, cols):
        return dot(nor_all[rows_of(half, k), :], w_in[:, cols], 1, 0)

    def grad_product(half, k, cols):
        return dot(cot_all[rows_of(half, k), :], w_full[:, cols], 1, 0)

    pres = [HiddenSum(0, half, pre_product) for half in range(2)]
    grads = [HiddenSum(1, half, grad_product) for half in range(2)]

    def across_three():
        across.onward(3)
        tok_to_core(3)
        tok_to_core(-3)

    def cots_two():
        cots.onward(2)

    normalise(0)
    load_w_in.wait()
    pres[0].begin([across_three, cots_two])
    near.onward(4)
    across.onward(4)
    tok_to_core(-4)
    normalise(1)
    pres[0].relayed()
    pres[1].begin([lambda: cots.onward(3)])
    pres[0].pair_up()
    cots.onward(4)
    pres[1].relayed()
    cots.finish(cot_all)
    for copy in turned:
        copy.wait_recv()
    load_w_out.wait()
    grads[0].begin()

    bias = b_in[:, pl.ds(pl.multiple_of(g * W, W), W)]

    class HiddenGather:
        def __init__(self, whole):
            self.whole, self.sides, self.onwards = whole, {}, []

        def begin(self, half):
            rows = self.whole.at[rows_of(half, x)]
            for side, step in enumerate((1, -1)):
                self.sides[side, half] = net.send(rows, rows, gz=x_dev(step))

        def onward(self):
            for side, step in enumerate((1, -1)):
                self.sides[side, side].wait_recv()
                rows = self.whole.at[rows_of(side, x_at(-step))]
                self.onwards.append(net.send(rows, rows, gz=x_dev(step)))

        def neighbours(self):
            for copy in self.sides.values():
                copy.wait_recv()

        def finish(self):
            for copy in self.onwards:
                copy.wait_recv()

    acts, pgs = HiddenGather(act_all), HiddenGather(pg_all)

    class FeatureSum:
        def __init__(self, n, product):
            self.n, self.product = n, product
            self.cores, self.three, self.four, self.last_hops = {}, {}, {}, {}

        def target(self, order):
            return lax.div(x, 2) if order == 0 else 1 - lax.div(x, 2)

        def products(self, order):
            n, j = self.n, self.target(order)

            def send_tile(cols):
                value = self.product(2 * j + (1 - c), cols)
                core_out[n, order, :, :, cols] = value.reshape(NZ, SH, TILE).astype(BF)

            tiles(send_tile)
            self.cores[order] = net.send(
                core_out.at[n, order], core_in.at[n, order], gy=core_peer
            )

            def keep_tile(cols):
                value = self.product(2 * j + c, cols)
                keep[n, order, :, :, cols] = value.reshape(NZ, SH, TILE)

            tiles(keep_tile)

        def scatter(self, order):
            n = self.n
            self.cores[order].wait_recv()

            def add_one(i, carry):
                value = keep[n, order, i] + core_in[n, order, i].astype(F32)
                keep[n, order, i] = value
                z_out[n, order, i] = value.astype(BF)
                return carry

            lax.fori_loop(0, NZ, add_one, 0)
            out, sides = z_out.at[n, order], tuple(enumerate((1, -1)))
            self.three[order] = [
                net.send(out.at[PLACE[3 * d]], z_three.at[n, order, i], gx=z_at(d))
                for i, d in sides
            ]
            self.four[order] = [
                net.send(
                    out.at[PLACE[4], :, part], z_four.at[n, order, i, :, part], gx=z_at(2 * d)
                )
                for (i, d), part in zip(sides, PARTS)
            ]
            self.last_hops[order] = [
                net.send(out.at[PLACE[d]], z_in.at[n, order, i], gx=z_at(d)) for i, d in sides
            ]

        def relay(self, order):
            n = self.n
            for i, d in enumerate((1, -1)):
                self.three[order][i].wait_recv()
                self.four[order][i].wait_recv()
                for k, part in enumerate(PARTS):
                    value = keep[n, order, PLACE[2 * d], :, part]
                    value = value + z_three[n, order, i, :, part].astype(F32)
                    if k == i:
                        value = value + z_four[n, order, i, :, part].astype(F32)
                    z_two[n, order, i, :, part] = value.astype(BF)
                self.last_hops[order].append(
                    net.send(z_two.at[n, order, i], z_in.at[n, order, 2 + i], gx=z_at(2 * d))
                )

        def collect(self, order):
            n = self.n
            for copy in self.last_hops[order]:
                copy.wait_recv()
            value = keep[n, order, 0]
            for s in range(4):
                value = value + z_in[n, order, s].astype(F32)
            total[n, order] = value

        def exchange(self):
            n = self.n
            here = lax.rem(lax.div(x, 2) + yl, 2)
            ty_out[n] = total[n, 1 - here].astype(BF)
            self.last = net.send(ty_out.at[n], ty_in.at[n], gy=y_peer)
            self.here = here

        def result(self):
            self.last.wait_recv()
            return total[self.n, self.here] + ty_in[self.n].astype(F32)

    ys = FeatureSum(0, lambda k, cols: dot(both_halves(act_all, k), w_full[cols, :], 1, 1))
    norms = FeatureSum(1, lambda k, cols: dot(both_halves(pg_all, k), w_in[cols, :], 1, 1))

    STEP = 32

    def activate(half):
        pres[half].pair.wait_recv()

        def one(i, carry):
            start = pl.multiple_of(i * STEP, STEP)
            rows = pl.ds(start, STEP)
            v = pres[half].total(rows) + bias
            t = jnp.tanh(ROOT * (v + CUBIC * v * v * v))
            place = pl.multiple_of(half * (4 * HALF) + x * HALF + start, STEP)
            act_all[pl.ds(place, STEP), :] = (0.5 * v * (1.0 + t)).astype(BF)
            pre[half, rows, :] = 0.5 * (1.0 + t) + 0.5 * v * (1.0 - t * t) * ROOT * (
                1.0 + 3.0 * CUBIC * v * v
            )
            return carry

        lax.fori_loop(0, HALF // STEP, one, 0)
        acts.begin(half)

    def backward(half):
        grads[half].pair.wait_recv()

        def one(i, carry):
            start = pl.multiple_of(i * STEP, STEP)
            rows = pl.ds(start, STEP)
            place = pl.multiple_of(half * (4 * HALF) + x * HALF + start, STEP)
            pg_all[pl.ds(place, STEP), :] = (
                grads[half].total(rows) * pre[half, rows, :]
            ).astype(BF)
            return carry

        lax.fori_loop(0, HALF // STEP, one, 0)
        pgs.begin(half)

    pres[1].pair_up()
    activate(0)
    grads[0].relayed()
    grads[1].begin()
    grads[0].pair_up()
    activate(1)
    grads[1].relayed()
    backward(0)
    grads[1].pair_up()
    acts.onward()
    acts.neighbours()
    ys.products(0)
    backward(1)
    ys.scatter(0)
    acts.finish()
    ys.products(1)

    def w_out_tile(rows):
        w_send[rows, :] = dot(cot_all[:, rows], act_all[...], 0, 0).astype(BF)

    tiles(w_out_tile)
    for s in range(1, 4):
        net.send(
            w_send.at[features_of(g_at(s))], w_out_grad.at[:, hidden_of(g)], gy=g_at(s)
        )
    net.local(w_send.at[features_of(g)], w_out_grad.at[:, hidden_of(g)])
    pgs.onward()
    ys.relay(0)
    ys.scatter(1)
    pgs.neighbours()
    norms.products(0)
    norms.scatter(0)
    ys.relay(1)
    pgs.finish()
    norms.products(1)
    norms.scatter(1)
    norms.relay(0)

    def bias_sum(i, carry):
        rows = pl.ds(pl.multiple_of(i * STEP, STEP), STEP)
        return carry + jnp.sum(pg_all[rows, :].astype(F32), 0, keepdims=True)

    b_grad[g] = lax.fori_loop(0, W // STEP, bias_sum, jnp.zeros((1, W), F32))
    biases = [net.send(b_grad.at[g], b_grad.at[g], gy=g_at(s)) for s in range(1, 4)]

    def w_in_tile(rows):
        w_in_out[rows, :] = dot(nor_all[:, rows], pg_all[...], 0, 0).astype(BF)

    tiles(w_in_tile)
    net.local(w_in_out, w_in_grad)

    norms.relay(1)
    ys.collect(0)
    ys.collect(1)
    ys.exchange()
    norms.collect(0)
    norms.collect(1)
    norms.exchange()
    partial = jnp.zeros((1, W), F32)
    for order in range(2):
        value = total[1, order]
        centred = centred_rows(norms.target(order), c, z)
        partial = partial + jnp.sum(value * centred, 0, keepdims=True)
        value = value * gain_row()
        stat2_out[order] = pack(
            jnp.sum(value, 1, keepdims=True), jnp.sum(value * centred, 1, keepdims=True)
        )
    mine, other = norms.here, 1 - norms.here
    stats2 = [
        net.send(stat2_out.at[mine], stat2_in.at[s], gz=q_at(s)) for s in range(1, NZ)
    ] + [
        net.send(stat2_out.at[other], stat2_in.at[NZ + s], gy=y_peer, gz=q_at(s))
        for s in range(NZ)
    ]
    stat2_in[0] = stat2_out[mine]
    gz_in[z] = partial
    gains = [net.send(gz_in.at[z], gz_in.at[z], gx=z_at(s)) for s in range(1, NZ)]
    y_out[...] = ys.result().astype(BF)

    norm_grad = norms.result()
    centred = centre()
    hat_grad = norm_grad * gain_row()
    for copy in gains:
        copy.wait_recv()
    value = gz_in[0]
    for i in range(1, NZ):
        value = value + gz_in[i]
    gy_in[g] = value
    gains = [net.send(gy_in.at[g], gy_in.at[g], gy=g_at(s)) for s in range(1, 4)]
    for copy in stats2:
        copy.wait_recv()
    packed = stat2_in[0]
    for s in range(1, 2 * NZ):
        packed = packed + stat2_in[s]
    first, second = unpack(packed)
    in_grad[...] = (
        (hat_grad - first / FEATURES - centred * (second / FEATURES)) * inv_std
    ).astype(BF)
    for copy in gains:
        copy.wait_recv()
    g_grad[...] = (gy_in[0] + gy_in[1]) + (gy_in[2] + gy_in[3])
    net.drain()


def hand_over(*refs):
    ins, outs, held, sems = refs[:6], refs[6:12], refs[12:17], refs[17]
    order = (2, 3, 0, 1, 4)
    first = {i: pltpu.make_async_copy(ins[i], held[i], sems.at[i]) for i in order}
    second = {i: pltpu.make_async_copy(held[i], outs[i], sems.at[5 + i]) for i in order}
    for i in order:
        first[i].start()
    outs[5][...] = ins[5][...].reshape(W)
    for i in order:
        first[i].wait()
        second[i].start()
    for i in order:
        second[i].wait()


def shards(tokens, gain, w_in, b_in, w_out, cotangent):
    vmem = pl.BlockSpec(memory_space=pltpu.VMEM)
    hbm = pl.BlockSpec(memory_space=pl.ANY)
    results = (
        jax.ShapeDtypeStruct((SH, W), BF),
        jax.ShapeDtypeStruct((SH, W), BF),
        jax.ShapeDtypeStruct((W, W), BF),
        jax.ShapeDtypeStruct((FB, 4 * W), BF),
        jax.ShapeDtypeStruct((4, 1, W), F32),
        jax.ShapeDtypeStruct((1, W), F32),
    )
    outs = pl.pallas_call(
        kernel,
        out_shape=results,
        in_specs=[vmem, vmem, hbm, vmem, hbm, vmem],
        out_specs=[vmem, vmem, hbm, hbm, vmem, vmem],
        scratch_shapes=[
            pltpu.VMEM((2, NZ, 2, SH, W), BF),
            pltpu.VMEM((2, NZ, 2, SH, W), BF),
            pltpu.VMEM((W, W), BF),
            pltpu.VMEM((W, W), BF),
            pltpu.VMEM((W, W), BF),
            pltpu.VMEM((W, W), BF),
            pltpu.VMEM((W, W), BF),
            pltpu.VMEM((W, W), BF),
            pltpu.VMEM((W, W), BF),
            pltpu.VMEM((W, W), BF),
            pltpu.VMEM((NZ, SH, LANES), F32),
            pltpu.VMEM((4, NZ, 1, LANES), F32),
            pltpu.VMEM((4, HALF, W), BF),
            pltpu.VMEM((4, 2, QUART, W), F32),
            pltpu.VMEM((4, 2, HALF, W), BF),
            pltpu.VMEM((4, HALF, W), F32),
            pltpu.VMEM((4, 2, QUART, W), BF),
            pltpu.VMEM((4, 2, HALF, W), BF),
            pltpu.VMEM((4, HALF, W), BF),
            pltpu.VMEM((4, HALF, W), BF),
            pltpu.VMEM((2, HALF, W), F32),
            pltpu.VMEM((2, 2, NZ, SH, W), F32),
            pltpu.VMEM((2, 2, NZ, SH, W), BF),
            pltpu.VMEM((2, 2, NZ, SH, W), BF),
            pltpu.VMEM((2, 2, NZ, SH, W), BF),
            pltpu.VMEM((2, 2, 4, SH, W), BF),
            pltpu.VMEM((2, 2, 2, SH, W), BF),
            pltpu.VMEM((2, 2, 2, SH, W), BF),
            pltpu.VMEM((2, 2, 2, SH, W), BF),
            pltpu.VMEM((2, 2, SH, W), F32),
            pltpu.VMEM((2, SH, W), BF),
            pltpu.VMEM((2, SH, W), BF),
            pltpu.VMEM((2 * NZ, 1, LANES), F32),
            pltpu.VMEM((2, 1, LANES), F32),
            pltpu.VMEM((NZ, 1, W), F32),
            pltpu.VMEM((4, 1, W), F32),
            pltpu.SemaphoreType.DMA((COPIES,)),
            pltpu.SemaphoreType.DMA((COPIES,)),
            pltpu.SemaphoreType.DMA((4,)),
        ],
        compiler_params=pltpu.CompilerParams(
            collective_id=0, has_side_effects=True, vmem_limit_bytes=58 << 20
        ),
        cost_estimate=pl.CostEstimate(
            flops=12 * W * W * W, bytes_accessed=10 * W * W, transcendentals=CH * W
        ),
    )(tokens, gain, w_in, b_in.reshape(1, 4 * W), w_out.T, cotangent)
    y_branch, input_grad, w_in_grad, w_out_grad, bias_grad, gain_grad = pl.pallas_call(
        hand_over,
        out_shape=results[:5] + (jax.ShapeDtypeStruct((W,), F32),),
        in_specs=[hbm] * 5 + [vmem],
        out_specs=[hbm] * 5 + [vmem],
        scratch_shapes=[pltpu.VMEM(one.shape, one.dtype) for one in results[:5]]
        + [pltpu.SemaphoreType.DMA((10,))],
    )(*outs)
    return (
        y_branch,
        input_grad,
        w_in_grad,
        w_out_grad.T,
        bias_grad.reshape(4 * W),
        gain_grad,
    )


def solution(mesh):
    placed = (
        P(("gy", "gx"), "gz"),
        P("gz"),
        P("gz", ("gx", "gy")),
        P("gx"),
        P("gx", ("gz", "gy")),
        P(("gy", "gx"), "gz"),
    )
    return jax.shard_map(
        shards,
        mesh=mesh,
        in_specs=placed,
        out_specs=(
            P(("gy", "gx"), "gz"),
            P(("gy", "gx"), "gz"),
            P("gz", ("gx", "gy")),
            P("gx", ("gz", "gy")),
            P("gx"),
            P("gz"),
        ),
        check_vma=False,
    )
```
